32 devices in a mesh: groups: 2 (over y), dp: 16 (over z, x, core), basis: 1.
Axes of the slice: x: 2, y: 2, z: 4, core: 2. Of those that a mesh axis runs over, the one named last changes fastest.
Arguments:
- factors_in: bfloat16 [128, 8192], P(('groups', 'dp'), 'basis'), parts along dimension 0, may hold values from -6 to 6
- factors_out: bfloat16 [128, 8192], P(('groups', 'dp'), 'basis'), parts along dimension 0, may hold values from -0.59765625 to 0.59765625
- basis_in: bfloat16 [8192, 8192], P('basis', 'dp'), may hold values from -0.0625 to 0.0625
- basis_out: bfloat16 [8192, 8192], P('basis', 'dp'), may hold values from -0.0625 to 0.0625
- eigvals: bfloat16 [8192, 8192], P('dp'), may hold values from 0.5 to 4
- live_counts: int32 [32], P(('groups', 'dp')), parts along dimension 0, may hold values from 1 to 4, 48 in all
Outputs:
- eigen_grads: bfloat16 [8, 8192, 8192], P(('groups', 'basis'), 'dp'), parts along dimension 0
The draws below stay inside these ranges and needn't reach their ends.
There are 2 independent parts, one for each index of `groups`. The reference program is written for one: setup_inputs(seed, part) draws one part's arguments, and reference() takes and returns one part's arrays. A program takes and returns all parts, laid end to end along the dimension named above; an argument that names none is the same for every part. Nothing has to cross between parts.
Inputs may be any that keep to these rules, and one draw needn't show every extreme that they name: `live_counts`: the live tokens of each dp index fill its first slots.
All inputs are finite; a program needn't handle non-finite values. No bound on the sum of `live_counts` on one device may be relied on, other than what follows from the above.
Results may differ from the reference program's by a relative error of at most 0.0057.
Values may be sent and summed in bfloat16 or wider, within the bound.
No kernel may reach another device: no remote copies, remote signals or barrier semaphores. Data moves between devices by JAX's collectives and lax.ppermute only.
A program may use at most 128 MiB of HBM per device.

```python
import math
import jax
import jax.numpy as jnp
import numpy as np
from jax import lax

D = 8192
TOK_DEV = 4
CAND = 4
TOKENS = 64
TOK = 16
N_DP = 16


def block_levels(own_key, dims, split, smallest, high):
    def one(dim, blocks):
        steps = jax.random.uniform(jax.random.fold_in(jax.random.fold_in(own_key, 6), dim), (blocks,), jnp.float32, smallest / len(split), high / len(split))
        return jnp.repeat(jnp.exp(steps), dims[dim] // blocks).reshape((-1,) + (1,) * (len(dims) - dim - 1))

    level = one(*split[0])
    for cut in split[1:]:
        level = level * one(*cut)
    return level


def length_profile(number_of, total, most, slope):
    portions = [(1 << 20) // math.isqrt(standing ** slope) + 1 for standing in range(2, number_of + 1)]
    rest, holding = total - most - (number_of - 1), [1] * (number_of - 1)
    while rest > 0:
        movable = [i for i in range(number_of - 1) if holding[i] < most]
        whole, left = sum([portions[i] for i in movable]), rest
        for i in movable:
            extra = min(most - holding[i], max(1, left * portions[i] // whole), rest)
            holding[i] = holding[i] + extra
            rest = rest - extra
    return np.array([most] + holding)


def uneven_parts(stream_key, count, total, limit, skew):
    if count == 2:
        one = jax.random.randint(stream_key, (), max(1, total - limit), min(limit, total - 1) + 1)
        return jnp.stack([one, total - one])
    tallies = jnp.asarray(length_profile(count, total, limit, skew), jnp.int32)
    couples = (count - 1) // 2
    giver, receiver = tallies[1:1 + 2 * couples:2], tallies[2:2 + 2 * couples:2]
    margin = jnp.minimum(giver - 1, limit - receiver)
    moved = jax.random.randint(jax.random.fold_in(stream_key, 1), (couples,), 0, 1 << 20) % (margin + 1)
    tallies = tallies.at[1:1 + 2 * couples:2].set(giver - moved).at[2:2 + 2 * couples:2].set(receiver + moved)
    return tallies[jax.random.permutation(jax.random.fold_in(stream_key, 2), count)]


def scatter_about(stream_key, dims, spread, bound, cuts=(), kind=jnp.bfloat16):
    drawn = spread * jax.random.normal(stream_key, dims, jnp.float32)
    if cuts:
        drawn = drawn * block_levels(stream_key, dims, cuts, -0.22, 0.18)
    return jnp.clip(drawn, -bound, bound).astype(kind)


def setup_inputs(seed: int = 0, part: int = 0) -> dict:
    streams_of = jax.random.split(jax.random.key(seed), 7)
    part_keys = jax.random.split(jax.random.fold_in(streams_of[6], part), 7)
    return {
        "factors_in": scatter_about(part_keys[0], (TOKENS, D), 1.0, 6.0, ((0, 16),)),
        "factors_out": scatter_about(part_keys[1], (TOKENS, D), 0.1, 0.59765625, ((0, 16),)),
        "basis_in": scatter_about(streams_of[2], (D, D), D ** -0.5, 0.0625, ((1, 16),)),
        "basis_out": scatter_about(streams_of[3], (D, D), D ** -0.5, 0.0625, ((1, 16),)),
        "eigvals": jnp.clip(jnp.exp(math.log(4.0) - 2.0794415 * jax.random.uniform(streams_of[4], (D, D), jnp.float32) ** block_levels(streams_of[4], (D, D), ((0, 16),), -0.2, 0.2)), 0.5, 4.0).astype(jnp.bfloat16),
        "live_counts": uneven_parts(part_keys[5], N_DP, 3 * N_DP * TOK_DEV // 4, TOK_DEV, 2).astype(jnp.int32),
    }


def reference(factors_in, factors_out, basis_in, basis_out, eigvals, live_counts):
    slots = jnp.arange(TOKENS, dtype=jnp.int32)
    owner = slots // TOK_DEV
    live = (slots % TOK_DEV) < live_counts[owner]
    masked = jnp.where(live[:, None], factors_in, jnp.zeros_like(factors_in))
    proj_in = jnp.dot(masked, basis_in, preferred_element_type=jnp.float32).astype(jnp.bfloat16)
    proj_out = jnp.dot(factors_out, basis_out, preferred_element_type=jnp.float32).astype(jnp.bfloat16)
    shifted = eigvals.astype(jnp.float32) + 0.01
    pin_all = proj_in.reshape(CAND, TOK, D)
    pout_all = proj_out.reshape(CAND, TOK, D)

    def one_candidate(pair):
        pout_c, pin_c = pair
        summed = jnp.dot(pout_c.T, pin_c, preferred_element_type=jnp.float32)
        return (summed / shifted).astype(jnp.bfloat16)

    return lax.map(one_candidate, (pout_all, pin_all))
```

```python
import functools

import jax
import jax.numpy as jnp
from jax import lax
from jax.experimental import pallas as pl
from jax.experimental.pallas import tpu as pltpu
from jax.sharding import PartitionSpec as P

CAND = 4
KBLK = 1024


def general(factors_in, factors_out, basis_in, basis_out, eigvals, live_counts):
    slot_rows = factors_in.shape[0]
    keep = (lax.iota(jnp.int32, slot_rows) < live_counts[0])[:, None]
    masked = jnp.where(keep, factors_in, jnp.zeros_like(factors_in))
    partial_in = jnp.dot(
        lax.all_gather(masked, "dp", axis=0, tiled=True),
        basis_in,
        preferred_element_type=jnp.float32,
    )
    partial_out = jnp.dot(
        lax.all_gather(factors_out, "dp", axis=0, tiled=True),
        basis_out,
        preferred_element_type=jnp.float32,
    )
    halves = lax.axis_size("basis")
    share = partial_in.shape[0] // halves
    summed_in, summed_out = lax.psum((partial_in, partial_out), "basis")
    first = lax.axis_index("basis") * share
    proj_in = lax.dynamic_slice_in_dim(summed_in, first, share, 0).astype(jnp.bfloat16)
    proj_out = lax.dynamic_slice_in_dim(summed_out, first, share, 0).astype(jnp.bfloat16)
    cand_local = CAND // halves
    per_cand = share // cand_local
    pout_grouped = proj_out.reshape(cand_local, per_cand, proj_out.shape[1])
    shifted = eigvals.astype(jnp.float32) + 0.01
    piece = lax.all_gather(proj_in, "dp", axis=1, tiled=True)
    pin_grouped = piece.reshape(cand_local, per_cand, piece.shape[1])
    summed = jnp.einsum(
        "ati,atj->aij", pout_grouped, pin_grouped, preferred_element_type=jnp.float32
    )
    return (summed / shifted[None, :, :]).astype(jnp.bfloat16)


def gather(x, n):
    def swap(y, m):
        return lax.ppermute(y, "dp", [(d, d ^ m) for d in range(n)])

    column = [x] + [swap(x, 4 * k) for k in range(1, n // 4)]
    pair = [swap(y, 2) for y in column]
    lane = [column, pair]
    other = [[swap(y, 1) for y in side] for side in lane]
    return [
        (other if m & 1 else lane)[(m >> 1) & 1][m >> 2] for m in range(n)
    ]


def project_kernel(n, own_ref, *refs):
    pieces, basis_ref, out_ref, rows, acc = refs[:n], refs[n], refs[n + 1], refs[n + 2], refs[n + 3]
    step = pl.program_id(0)
    width = basis_ref.shape[0]
    at = pl.multiple_of(step * width, width)
    slots = pieces[0].shape[0]
    for m in range(n):
        rows[m * slots:(m + 1) * slots, :] = pieces[m][:, pl.ds(at, width)].astype(jnp.float32)
    part = jnp.dot(
        rows[...].astype(jnp.bfloat16), basis_ref[...], preferred_element_type=jnp.float32
    )

    @pl.when(step == 0)
    def _():
        acc[...] = part

    @pl.when(step > 0)
    def _():
        acc[...] += part

    @pl.when(step == pl.num_programs(0) - 1)
    def _():
        total = n * slots
        to = lax.broadcasted_iota(jnp.int32, (total, total), 0)
        held = lax.broadcasted_iota(jnp.int32, (total, total), 1)
        where = jnp.bitwise_xor(held // slots, own_ref[0]) * slots + held % slots
        pick = jnp.where(to == where, 1.0, 0.0).astype(jnp.bfloat16)
        out_ref[...] = jnp.dot(
            pick, acc[...].astype(jnp.bfloat16), preferred_element_type=jnp.float32
        ).astype(jnp.bfloat16)


def project(own, pieces, basis):
    n = len(pieces)
    slots, depth = pieces[0].shape
    cols = basis.shape[1]
    return pl.pallas_call(
        functools.partial(project_kernel, n),
        out_shape=jax.ShapeDtypeStruct((n * slots, cols), jnp.bfloat16),
        grid_spec=pltpu.PrefetchScalarGridSpec(
            num_scalar_prefetch=1,
            grid=(depth // KBLK,),
            in_specs=[pl.BlockSpec((slots, depth), lambda k, own: (0, 0))] * n
            + [pl.BlockSpec((KBLK, cols), lambda k, own: (k, 0))],
            out_specs=pl.BlockSpec((n * slots, cols), lambda k, own: (0, 0)),
            scratch_shapes=[
                pltpu.VMEM((n * slots, KBLK), jnp.float32),
                pltpu.VMEM((n * slots, cols), jnp.float32),
            ],
        ),
        compiler_params=pltpu.CompilerParams(vmem_limit_bytes=24 << 20),
        cost_estimate=pl.CostEstimate(
            flops=2 * n * slots * depth * cols,
            bytes_accessed=2 * depth * (cols + n * slots),
            transcendentals=0,
        ),
    )(own, *pieces, basis)


def outer_kernel(n, own_ref, *refs):
    pieces, pout_ref, eig_ref, out_ref, left, held = refs[:n], *refs[n:]
    step = pl.program_id(0)
    total = pout_ref.shape[0]
    per_cand = total // CAND

    @pl.when(step == 0)
    def _():
        turned = pout_ref[...].astype(jnp.float32).T
        slot = lax.broadcasted_iota(jnp.int32, turned.shape, 1)
        for c in range(CAND):
            left[c] = jnp.where(slot // per_cand == c, turned, 0.0).astype(jnp.bfloat16)

    for m in range(n):
        @pl.when(step == m)
        def _():
            held[...] = pieces[m][...]

    scale = 1.0 / (eig_ref[...].astype(jnp.float32) + 0.01)
    for c in range(CAND):
        summed = jnp.dot(left[c], held[...], preferred_element_type=jnp.float32)
        out_ref[c] = (summed * scale).astype(jnp.bfloat16)


def outer(own, pieces, pout, eigvals):
    n = len(pieces)
    total, cols = pieces[0].shape
    rows, width = eigvals.shape
    return pl.pallas_call(
        functools.partial(outer_kernel, n),
        out_shape=jax.ShapeDtypeStruct((CAND, rows, width), jnp.bfloat16),
        grid_spec=pltpu.PrefetchScalarGridSpec(
            num_scalar_prefetch=1,
            grid=(n,),
            in_specs=[pl.BlockSpec((total, cols), lambda m, own: (0, 0))] * n
            + [
                pl.BlockSpec((total, rows), lambda m, own: (0, 0)),
                pl.BlockSpec((rows, cols), lambda m, own: (0, jnp.bitwise_xor(m, own[0]))),
            ],
            out_specs=pl.BlockSpec(
                (CAND, rows, cols), lambda m, own: (0, 0, jnp.bitwise_xor(m, own[0]))
            ),
            scratch_shapes=[
                pltpu.VMEM((CAND, rows, total), jnp.bfloat16),
                pltpu.VMEM((total, cols), jnp.bfloat16),
            ],
        ),
        compiler_params=pltpu.CompilerParams(vmem_limit_bytes=32 << 20),
        cost_estimate=pl.CostEstimate(
            flops=2 * total * rows * width,
            bytes_accessed=2 * rows * width * (CAND + 1),
            transcendentals=rows * width,
        ),
    )(own, *pieces, pout, eigvals)


def by_swaps(factors_in, factors_out, basis_in, basis_out, eigvals, live_counts):
    n = lax.axis_size("dp")
    own = lax.axis_index("dp").astype(jnp.int32)[None]
    slots = factors_in.shape[0]
    pin = project(own, gather(factors_in, n), basis_in)
    keep = (lax.iota(jnp.int32, slots) < live_counts[0])[:, None]
    masked = jnp.where(keep, factors_out, jnp.zeros_like(factors_out))
    pout = project(own, gather(masked, n), basis_out)
    return outer(own, gather(pin, n), pout, eigvals)


def solution(mesh):
    placed = (
        P(("groups", "dp"), "basis"),
        P(("groups", "dp"), "basis"),
        P("basis", "dp"),
        P("basis", "dp"),
        P("dp", None),
        P(("groups", "dp")),
    )
    chosen = by_swaps if mesh.shape["basis"] == 1 and mesh.shape["dp"] == 16 else general
    return jax.shard_map(
        chosen,
        mesh=mesh,
        in_specs=placed,
        out_specs=P(("groups", "basis"), "dp", None),
        check_vma=False,
    )
```

```python
import functools

import jax
import jax.numpy as jnp
from jax import lax
from jax.experimental import pallas as pl
from jax.experimental.pallas import tpu as pltpu
from jax.sharding import PartitionSpec as P

CAND = 4
KBLK = 1024
RBLK = 128
VMEM = 50 << 20


def general(factors_in, factors_out, basis_in, basis_out, eigvals, live_counts):
    slot_rows = factors_in.shape[0]
    keep = (lax.iota(jnp.int32, slot_rows) < live_counts[0])[:, None]
    masked = jnp.where(keep, factors_in, jnp.zeros_like(factors_in))
    partial_in = jnp.dot(
        lax.all_gather(masked, "dp", axis=0, tiled=True),
        basis_in,
        preferred_element_type=jnp.float32,
    )
    partial_out = jnp.dot(
        lax.all_gather(factors_out, "dp", axis=0, tiled=True),
        basis_out,
        preferred_element_type=jnp.float32,
    )
    halves = lax.axis_size("basis")
    share = partial_in.shape[0] // halves
    summed_in, summed_out = lax.psum((partial_in, partial_out), "basis")
    first = lax.axis_index("basis") * share
    proj_in = lax.dynamic_slice_in_dim(summed_in, first, share, 0).astype(jnp.bfloat16)
    proj_out = lax.dynamic_slice_in_dim(summed_out, first, share, 0).astype(jnp.bfloat16)
    cand_local = CAND // halves
    per_cand = share // cand_local
    pout_grouped = proj_out.reshape(cand_local, per_cand, proj_out.shape[1])
    shifted = eigvals.astype(jnp.float32) + 0.01
    piece = lax.all_gather(proj_in, "dp", axis=1, tiled=True)
    pin_grouped = piece.reshape(cand_local, per_cand, piece.shape[1])
    summed = jnp.einsum(
        "ati,atj->aij", pout_grouped, pin_grouped, preferred_element_type=jnp.float32
    )
    return (summed / shifted[None, :, :]).astype(jnp.bfloat16)


def swap(x, m):
    n = lax.axis_size("dp")
    return lax.ppermute(x, "dp", [(d, d ^ m) for d in range(n)])


def gather(x, n):
    column = [x] + [swap(x, 4 * k) for k in range(1, n // 4)]
    pair = [swap(y, 2) for y in column]
    lane = [column, pair]
    other = [[swap(y, 1) for y in side] for side in lane]
    return [(other if m & 1 else lane)[(m >> 1) & 1][m >> 2] for m in range(n)]


def project_kernel(n, first, turn, own_ref, *refs):
    pieces, (basis_ref, out_ref, acc) = refs[:n], refs[n:]
    step = pl.program_id(0)
    width = basis_ref.shape[0]
    at = pl.multiple_of(step * width, width)
    held = pieces[0].shape[0]
    slots = held // 2
    rows = jnp.concatenate(
        [piece[:, pl.ds(at, width)].astype(jnp.float32) for piece in pieces], axis=0
    ).astype(jnp.bfloat16)
    part = jnp.dot(rows, basis_ref[...], preferred_element_type=jnp.float32)

    @pl.when(step == 0)
    def _():
        acc[...] = part

    @pl.when(step > 0)
    def _():
        acc[...] += part

    @pl.when(step == pl.num_programs(0) - 1)
    def _():
        total = n * slots
        to = lax.broadcasted_iota(jnp.int32, (total, n * held), 0)
        come = lax.broadcasted_iota(jnp.int32, (total, n * held), 1)
        slot = come % held - first
        where = jnp.bitwise_xor(come // held, own_ref[0]) * slots + slot
        chosen = (to == where) & (slot >= 0) & (slot < slots)
        pick = jnp.where(chosen, 1.0, 0.0).astype(jnp.bfloat16)
        proj = jnp.dot(pick, acc[...].astype(jnp.bfloat16), preferred_element_type=jnp.float32)
        if turn:
            turned = proj.T
            token = lax.broadcasted_iota(jnp.int32, turned.shape, 1)
            for c in range(CAND):
                own_tokens = token // (total // CAND) == c
                out_ref[c] = jnp.where(own_tokens, turned, 0.0).astype(jnp.bfloat16)
        else:
            out_ref[...] = proj.astype(jnp.bfloat16)


def project(own, pieces, basis, first, turn):
    n = len(pieces)
    held, depth = pieces[0].shape
    cols = basis.shape[1]
    total = n * held // 2
    shape = (CAND, cols, total) if turn else (total, cols)
    return pl.pallas_call(
        functools.partial(project_kernel, n, first, turn),
        out_shape=jax.ShapeDtypeStruct(shape, jnp.bfloat16),
        grid_spec=pltpu.PrefetchScalarGridSpec(
            num_scalar_prefetch=1,
            grid=(depth // KBLK,),
            in_specs=[pl.BlockSpec((held, depth), lambda k, own: (0, 0))] * n
            + [pl.BlockSpec((KBLK, cols), lambda k, own: (k, 0))],
            out_specs=pl.BlockSpec(shape, lambda k, own: (0,) * len(shape)),
            scratch_shapes=[pltpu.VMEM((n * held, cols), jnp.float32)],
        ),
        compiler_params=pltpu.CompilerParams(vmem_limit_bytes=VMEM),
        cost_estimate=pl.CostEstimate(
            flops=2 * n * held * depth * cols,
            bytes_accessed=2 * depth * cols,
            transcendentals=0,
        ),
    )(own, *pieces, basis)


def outer_kernel(blocks, own_ref, *refs):
    count = len(blocks)
    pieces, (left_ref, eig_ref, *_, out_ref, held) = refs[:count], refs[count:]
    step = pl.program_id(0)
    at = 0
    for piece, (_, entries) in zip(pieces, blocks):
        for e in range(len(entries)):
            @pl.when(step == at)
            def _(piece=piece, e=e):
                held[...] = piece[...] if len(piece.shape) == 2 else piece[e]

            at += 1
    right = held[...]
    rows = out_ref.shape[1]
    for r in range(0, rows, RBLK):
        scale = 1.0 / (eig_ref[r:r + RBLK, :].astype(jnp.float32) + 0.01)
        for c in range(CAND):
            summed = jnp.dot(left_ref[c, r:r + RBLK, :], right, preferred_element_type=jnp.float32)
            out_ref[c, r:r + RBLK, :] = (summed * scale).astype(jnp.bfloat16)


def outer(own, blocks, left, eigvals, before):
    total, cols = blocks[0][0].shape[-2:]
    rows, width = eigvals.shape
    order = [m for _, entries in blocks for m in entries]

    def place(s, own):
        m = jnp.int32(order[0])
        for k in range(1, len(order)):
            m = jnp.where(s == k, order[k], m)
        return jnp.bitwise_xor(m, own[0])

    def whole(shape):
        return pl.BlockSpec(shape, lambda s, own: (0,) * len(shape))

    operands = [own] + [x for x, _ in blocks] + [left, eigvals]
    in_specs = [whole(x.shape) for x, _ in blocks] + [
        whole(left.shape),
        pl.BlockSpec((rows, cols), lambda s, own: (0, place(s, own))),
    ]
    aliases = {}
    if before is not None:
        aliases = {len(operands): 0}
        operands.append(before)
        in_specs.append(pl.BlockSpec(memory_space=pl.ANY))
    share = len(order) * cols
    return pl.pallas_call(
        functools.partial(outer_kernel, [(None, e) for _, e in blocks]),
        out_shape=jax.ShapeDtypeStruct((CAND, rows, width), jnp.bfloat16),
        grid_spec=pltpu.PrefetchScalarGridSpec(
            num_scalar_prefetch=1,
            grid=(len(order),),
            in_specs=in_specs,
            out_specs=pl.BlockSpec((CAND, rows, cols), lambda s, own: (0, 0, place(s, own))),
            scratch_shapes=[pltpu.VMEM((total, cols), jnp.bfloat16)],
        ),
        input_output_aliases=aliases,
        compiler_params=pltpu.CompilerParams(vmem_limit_bytes=VMEM),
        cost_estimate=pl.CostEstimate(
            flops=2 * total * rows * share,
            bytes_accessed=2 * rows * share * (CAND + 1),
            transcendentals=rows * share,
        ),
    )(*operands)


def by_swaps(factors_in, factors_out, basis_in, basis_out, eigvals, live_counts):
    n = lax.axis_size("dp")
    own = lax.axis_index("dp").astype(jnp.int32)[None]
    slots = factors_in.shape[0]
    keep = (lax.iota(jnp.int32, slots) < live_counts[0])[:, None]
    masked = jnp.where(keep, factors_out, jnp.zeros_like(factors_out))
    pieces = gather(jnp.concatenate([factors_in, masked], axis=0), n)
    pin = project(own, pieces, basis_in, 0, False)
    left = project(own, pieces, basis_out, slots, True)

    up = range(4, n, 4)
    core, pair = swap(pin, 1), swap(pin, 2)
    column = [swap(pin, m) for m in up]
    stacked = jnp.stack(column)
    stacked_pair = swap(stacked, 2)
    stacked_core = swap(stacked, 1)
    pair_core = swap(pair, 1)
    last = swap(stacked_pair, 1)
    out = outer(own, [(pin, [0]), (core, [1])], left, eigvals, None)
    out = outer(
        own, [(pair, [2])] + [(x, [m]) for x, m in zip(column, up)], left, eigvals, out
    )
    out = outer(
        own,
        [
            (pair_core, [3]),
            (stacked_core, [m + 1 for m in up]),
            (stacked_pair, [m + 2 for m in up]),
        ],
        left,
        eigvals,
        out,
    )
    return outer(own, [(last, [m + 3 for m in up])], left, eigvals, out)


def solution(mesh):
    placed = (
        P(("groups", "dp"), "basis"),
        P(("groups", "dp"), "basis"),
        P("basis", "dp"),
        P("basis", "dp"),
        P("dp", None),
        P(("groups", "dp")),
    )
    chosen = by_swaps if mesh.shape["basis"] == 1 and mesh.shape["dp"] == 16 else general
    return jax.shard_map(
        chosen,
        mesh=mesh,
        in_specs=placed,
        out_specs=P(("groups", "basis"), "dp", None),
        check_vma=False,
    )
```

```python
import functools

import jax
import jax.numpy as jnp
from jax import lax
from jax.experimental import pallas as pl
from jax.experimental.pallas import tpu as pltpu
from jax.sharding import PartitionSpec as P

CAND = 4
KBLK = 1024
RBLK = 128
VMEM = 50 << 20


def general(factors_in, factors_out, basis_in, basis_out, eigvals, live_counts):
    slot_rows = factors_in.shape[0]
    keep = (lax.iota(jnp.int32, slot_rows) < live_counts[0])[:, None]
    masked = jnp.where(keep, factors_in, jnp.zeros_like(factors_in))
    partial_in = jnp.dot(
        lax.all_gather(masked, "dp", axis=0, tiled=True),
        basis_in,
        preferred_element_type=jnp.float32,
    )
    partial_out = jnp.dot(
        lax.all_gather(factors_out, "dp", axis=0, tiled=True),
        basis_out,
        preferred_element_type=jnp.float32,
    )
    halves = lax.axis_size("basis")
    share = partial_in.shape[0] // halves
    summed_in, summed_out = lax.psum((partial_in, partial_out), "basis")
    first = lax.axis_index("basis") * share
    proj_in = lax.dynamic_slice_in_dim(summed_in, first, share, 0).astype(jnp.bfloat16)
    proj_out = lax.dynamic_slice_in_dim(summed_out, first, share, 0).astype(jnp.bfloat16)
    cand_local = CAND // halves
    per_cand = share // cand_local
    pout_grouped = proj_out.reshape(cand_local, per_cand, proj_out.shape[1])
    shifted = eigvals.astype(jnp.float32) + 0.01
    piece = lax.all_gather(proj_in, "dp", axis=1, tiled=True)
    pin_grouped = piece.reshape(cand_local, per_cand, piece.shape[1])
    summed = jnp.einsum(
        "ati,atj->aij", pout_grouped, pin_grouped, preferred_element_type=jnp.float32
    )
    return (summed / shifted[None, :, :]).astype(jnp.bfloat16)


def swap(x, m):
    n = lax.axis_size("dp")
    return lax.ppermute(x, "dp", [(d, d ^ m) for d in range(n)])


def after(x, *others):
    return lax.optimization_barrier((x,) + others)[0]


def flat(pieces, blocks):
    return [
        (piece, e if stacked else None, m)
        for piece, (stacked, entries) in zip(pieces, blocks)
        for e, m in enumerate(entries)
    ]


def shape_of(blocks):
    return tuple((x.ndim == 3, tuple(entries)) for x, entries in blocks)


def project_kernel(n, blocks, turn, own_ref, *refs):
    pieces, (basis_ref, out_ref, held, rows, acc, sems) = refs[:len(blocks)], refs[len(blocks):]
    step = pl.program_id(0)
    width = held.shape[1]
    at = pl.multiple_of(step * width, width)
    slots = pieces[0].shape[-2]

    @pl.when(step == 0)
    def _():
        for k in range(held.shape[0]):
            pltpu.make_async_copy(
                basis_ref.at[pl.ds(k * width, width)], held.at[k], sems.at[k]
            ).start()

    for piece, e, m in flat(pieces, blocks):
        part = piece[:, pl.ds(at, width)] if e is None else piece[e, :, pl.ds(at, width)]
        rows[m * slots:(m + 1) * slots, :] = part.astype(jnp.float32)
    pltpu.make_async_copy(basis_ref.at[pl.ds(at, width)], held.at[step], sems.at[step]).wait()
    part = jnp.dot(
        rows[...].astype(jnp.bfloat16), held[step], preferred_element_type=jnp.float32
    )

    @pl.when(step == 0)
    def _():
        acc[...] = part

    @pl.when(step > 0)
    def _():
        acc[...] += part

    @pl.when(step == pl.num_programs(0) - 1)
    def _():
        total = n * slots
        to = lax.broadcasted_iota(jnp.int32, (total, total), 0)
        come = lax.broadcasted_iota(jnp.int32, (total, total), 1)
        where = jnp.bitwise_xor(come // slots, own_ref[0]) * slots + come % slots
        pick = jnp.where(to == where, 1.0, 0.0).astype(jnp.bfloat16)
        proj = jnp.dot(pick, acc[...].astype(jnp.bfloat16), preferred_element_type=jnp.float32)
        if turn:
            turned = proj.T
            token = lax.broadcasted_iota(jnp.int32, turned.shape, 1)
            for c in range(CAND):
                own_tokens = token // (total // CAND) == c
                out_ref[c] = jnp.where(own_tokens, turned, 0.0).astype(jnp.bfloat16)
        else:
            out_ref[...] = proj.astype(jnp.bfloat16)


def whole(shape):
    return pl.BlockSpec(shape, lambda s, own: (0,) * len(shape))


def project(own, n, blocks, basis, turn):
    slots = blocks[0][0].shape[-2]
    depth, cols = basis.shape
    total = n * slots
    shape = (CAND, cols, total) if turn else (total, cols)
    steps = depth // KBLK
    return pl.pallas_call(
        functools.partial(project_kernel, n, shape_of(blocks), turn),
        out_shape=jax.ShapeDtypeStruct(shape, jnp.bfloat16),
        grid_spec=pltpu.PrefetchScalarGridSpec(
            num_scalar_prefetch=1,
            grid=(steps,),
            in_specs=[whole(x.shape) for x, _ in blocks] + [pl.BlockSpec(memory_space=pl.ANY)],
            out_specs=whole(shape),
            scratch_shapes=[
                pltpu.VMEM((steps, KBLK, cols), jnp.bfloat16),
                pltpu.VMEM((total, KBLK), jnp.float32),
                pltpu.VMEM((total, cols), jnp.float32),
                pltpu.SemaphoreType.DMA((steps,)),
            ],
        ),
        compiler_params=pltpu.CompilerParams(vmem_limit_bytes=VMEM),
        cost_estimate=pl.CostEstimate(
            flops=2 * total * depth * cols,
            bytes_accessed=2 * depth * cols,
            transcendentals=0,
        ),
    )(own, *[x for x, _ in blocks], basis)


def outer_kernel(blocks, own_ref, *refs):
    pieces = refs[:len(blocks)]
    left_ref, eig_ref, out_ref, right, eig, out, eig_sems, out_sems = (
        *refs[len(blocks):len(blocks) + 2], *refs[-6:]
    )
    listed = flat(pieces, blocks)
    count = len(listed)
    step = pl.program_id(0)
    rows, cols = eig.shape[1:]

    def columns(s):
        m = jnp.int32(listed[0][2])
        for k in range(1, count):
            m = jnp.where(s == k, listed[k][2], m)
        return pl.ds(pl.multiple_of(jnp.bitwise_xor(m, own_ref[0]) * cols, cols), cols)

    def read(s):
        return pltpu.make_async_copy(eig_ref.at[:, columns(s)], eig.at[s], eig_sems.at[s])

    def write(s, c):
        slot = lax.rem(s, 2)
        return pltpu.make_async_copy(
            out.at[slot, c], out_ref.at[c, :, columns(s)], out_sems.at[slot, c]
        )

    @pl.when(step == 0)
    def _():
        for s in range(count):
            read(s).start()

    for k, (piece, e, _) in enumerate(listed):
        @pl.when(step == k)
        def _(piece=piece, e=e):
            right[...] = piece[...] if e is None else piece[e]

    read(step).wait()
    slot = lax.rem(step, 2)
    for c in range(CAND):
        @pl.when(step >= 2)
        def _(c=c):
            write(step - 2, c).wait()

    for r in range(0, rows, RBLK):
        scale = 1.0 / (eig[step, r:r + RBLK, :].astype(jnp.float32) + 0.01)
        for c in range(CAND):
            summed = jnp.dot(
                left_ref[c, r:r + RBLK, :], right[...], preferred_element_type=jnp.float32
            )
            out[slot, c, r:r + RBLK, :] = (summed * scale).astype(jnp.bfloat16)
    for c in range(CAND):
        write(step, c).start()

    @pl.when(step == count - 1)
    def _():
        for s in range(max(0, count - 2), count):
            for c in range(CAND):
                write(s, c).wait()


def outer(own, blocks, left, eigvals, before):
    total, cols = blocks[0][0].shape[-2:]
    rows, width = eigvals.shape
    count = sum(len(entries) for _, entries in blocks)
    operands = [own] + [x for x, _ in blocks] + [left, eigvals]
    in_specs = [whole(x.shape) for x, _ in blocks] + [
        whole(left.shape),
        pl.BlockSpec(memory_space=pl.ANY),
    ]
    aliases = {}
    if before is not None:
        aliases = {len(operands): 0}
        operands.append(before)
        in_specs.append(pl.BlockSpec(memory_space=pl.ANY))
    share = count * cols
    return pl.pallas_call(
        functools.partial(outer_kernel, shape_of(blocks)),
        out_shape=jax.ShapeDtypeStruct((CAND, rows, width), jnp.bfloat16),
        grid_spec=pltpu.PrefetchScalarGridSpec(
            num_scalar_prefetch=1,
            grid=(count,),
            in_specs=in_specs,
            out_specs=pl.BlockSpec(memory_space=pl.ANY),
            scratch_shapes=[
                pltpu.VMEM((total, cols), jnp.bfloat16),
                pltpu.VMEM((count, rows, cols), jnp.bfloat16),
                pltpu.VMEM((2, CAND, rows, cols), jnp.bfloat16),
                pltpu.SemaphoreType.DMA((count,)),
                pltpu.SemaphoreType.DMA((2, CAND)),
            ],
        ),
        input_output_aliases=aliases,
        compiler_params=pltpu.CompilerParams(vmem_limit_bytes=VMEM),
        cost_estimate=pl.CostEstimate(
            flops=2 * total * rows * share,
            bytes_accessed=2 * rows * share * (CAND + 1),
            transcendentals=rows * share,
        ),
    )(*operands)


def by_swaps(factors_in, factors_out, basis_in, basis_out, eigvals, live_counts):
    n = lax.axis_size("dp")
    own = lax.axis_index("dp").astype(jnp.int32)[None]
    slots = factors_in.shape[0]
    column = (0, 4, 8, 12)
    pair = (2, 6, 10, 14)
    core = (1, 5, 9, 13)
    other = (3, 7, 11, 15)

    def send(x):
        return swap(x, 4), swap(x, 2), swap(x, 8), swap(x, 12)

    a = factors_in
    a1, ap, a2, a3 = send(a)
    keep = (lax.iota(jnp.int32, slots) < live_counts[0])[:, None]
    b = jnp.where(keep, factors_out, jnp.zeros_like(factors_out))
    a1, ap = lax.optimization_barrier((a1, ap))
    ap1 = swap(a1, 2)
    b, a2, a3 = lax.optimization_barrier((b, a2, a3))
    ap23 = swap(jnp.stack([a2, a3]), 2)
    a_column = jnp.stack([a, a1, a2, a3])
    a_core = swap(a_column, 1)
    b1, bp, b2, b3 = send(b)
    a_pair = jnp.stack([ap, ap1, ap23[0], ap23[1]])
    a_other = swap(a_pair, 1)
    b1, b2, b3, bp = lax.optimization_barrier((b1, b2, b3, bp, a_pair))[:4]
    b_column = jnp.stack([b, b1, b2, b3])
    bp123 = swap(b_column[1:], 2)
    b_core = swap(b_column, 1)
    pin = project(
        own, n, [(a_column, column), (a_pair, pair), (a_core, core), (a_other, other)],
        basis_in, False,
    )

    g1, gp, g2, g3 = send(pin)
    b_pair = jnp.concatenate([after(bp, pin)[None], bp123])
    b_other = swap(b_pair, 1)
    left = project(
        own, n, [(b_column, column), (b_pair, pair), (b_core, core), (b_other, other)],
        basis_out, True,
    )
    g1, g2, g3, gp = lax.optimization_barrier((g1, g2, g3, gp, left))[:4]
    g_column = jnp.stack([pin, g1, g2, g3])
    gp123 = swap(g_column[1:], 2)
    g_core = swap(g_column, 1)
    out = outer(own, [(g_column, column)], left, eigvals, None)
    g_pair = jnp.concatenate([gp[None], after(gp123, out)])
    g_other = swap(g_pair, 1)
    out = outer(own, [(g_core, core), (g_pair, pair)], left, eigvals, out)
    return outer(own, [(g_other, other)], left, eigvals, out)


def solution(mesh):
    placed = (
        P(("groups", "dp"), "basis"),
        P(("groups", "dp"), "basis"),
        P("basis", "dp"),
        P("basis", "dp"),
        P("dp", None),
        P(("groups", "dp")),
    )
    chosen = by_swaps if mesh.shape["basis"] == 1 and mesh.shape["dp"] == 16 else general
    return jax.shard_map(
        chosen,
        mesh=mesh,
        in_specs=placed,
        out_specs=P(("groups", "basis"), "dp", None),
        check_vma=False,
    )
```

```python
import functools

import jax
import jax.numpy as jnp
from jax import lax
from jax.experimental import pallas as pl
from jax.experimental.pallas import tpu as pltpu
from jax.sharding import PartitionSpec as P

CAND = 4
KBLK = 1024
RBLK = 256
FLIGHT = 3
VMEM = 50 << 20


def general(factors_in, factors_out, basis_in, basis_out, eigvals, live_counts):
    slot_rows = factors_in.shape[0]
    keep = (lax.iota(jnp.int32, slot_rows) < live_counts[0])[:, None]
    masked = jnp.where(keep, factors_in, jnp.zeros_like(factors_in))
    partial_in = jnp.dot(
        lax.all_gather(masked, "dp", axis=0, tiled=True),
        basis_in,
        preferred_element_type=jnp.float32,
    )
    partial_out = jnp.dot(
        lax.all_gather(factors_out, "dp", axis=0, tiled=True),
        basis_out,
        preferred_element_type=jnp.float32,
    )
    halves = lax.axis_size("basis")
    share = partial_in.shape[0] // halves
    summed_in, summed_out = lax.psum((partial_in, partial_out), "basis")
    first = lax.axis_index("basis") * share
    proj_in = lax.dynamic_slice_in_dim(summed_in, first, share, 0).astype(jnp.bfloat16)
    proj_out = lax.dynamic_slice_in_dim(summed_out, first, share, 0).astype(jnp.bfloat16)
    cand_local = CAND // halves
    per_cand = share // cand_local
    pout_grouped = proj_out.reshape(cand_local, per_cand, proj_out.shape[1])
    shifted = eigvals.astype(jnp.float32) + 0.01
    piece = lax.all_gather(proj_in, "dp", axis=1, tiled=True)
    pin_grouped = piece.reshape(cand_local, per_cand, piece.shape[1])
    summed = jnp.einsum(
        "ati,atj->aij", pout_grouped, pin_grouped, preferred_element_type=jnp.float32
    )
    return (summed / shifted[None, :, :]).astype(jnp.bfloat16)


def swap(x, m):
    n = lax.axis_size("dp")
    return lax.ppermute(x, "dp", [(d, d ^ m) for d in range(n)])


def after(x, *others):
    return lax.optimization_barrier((x,) + others)[0]


def flat(pieces, blocks):
    return [
        (piece, e if stacked else None, m)
        for piece, (stacked, entries) in zip(pieces, blocks)
        for e, m in enumerate(entries)
    ]


def shape_of(blocks):
    return tuple((x.ndim == 3, tuple(entries)) for x, entries in blocks)


def project_kernel(n, blocks, turn, own_ref, *refs):
    count = len(blocks)
    sources, basis_ref, out_ref = refs[:count], refs[count], refs[count + 1]
    pieces, (held, rows, acc, sems, piece_sems) = refs[count + 2:-5], refs[-5:]
    step = pl.program_id(0)
    width = held.shape[1]
    at = pl.multiple_of(step * width, width)
    slots = pieces[0].shape[-2]

    @pl.when(step == 0)
    def _():
        copies = [
            pltpu.make_async_copy(source, piece, piece_sems.at[k])
            for k, (source, piece) in enumerate(zip(sources, pieces))
        ]
        for k in range(held.shape[0]):
            pltpu.make_async_copy(
                basis_ref.at[pl.ds(k * width, width)], held.at[k], sems.at[k]
            ).start()
            if k == 0:
                for copy in copies:
                    copy.start()
        for copy in copies:
            copy.wait()

    for piece, e, m in flat(pieces, blocks):
        part = piece[:, pl.ds(at, width)] if e is None else piece[e, :, pl.ds(at, width)]
        rows[m * slots:(m + 1) * slots, :] = part.astype(jnp.float32)
    pltpu.make_async_copy(basis_ref.at[pl.ds(at, width)], held.at[step], sems.at[step]).wait()
    part = jnp.dot(
        rows[...].astype(jnp.bfloat16), held[step], preferred_element_type=jnp.float32
    )

    @pl.when(step == 0)
    def _():
        acc[...] = part

    @pl.when(step > 0)
    def _():
        acc[...] += part

    @pl.when(step == pl.num_programs(0) - 1)
    def _():
        total = n * slots
        to = lax.broadcasted_iota(jnp.int32, (total, total), 0)
        come = lax.broadcasted_iota(jnp.int32, (total, total), 1)
        where = jnp.bitwise_xor(come // slots, own_ref[0]) * slots + come % slots
        pick = jnp.where(to == where, 1.0, 0.0).astype(jnp.bfloat16)
        proj = jnp.dot(pick, acc[...].astype(jnp.bfloat16), preferred_element_type=jnp.float32)
        if turn:
            turned = proj.T
            token = lax.broadcasted_iota(jnp.int32, turned.shape, 1)
            for c in range(CAND):
                own_tokens = token // (total // CAND) == c
                out_ref[c] = jnp.where(own_tokens, turned, 0.0).astype(jnp.bfloat16)
        else:
            out_ref[...] = proj.astype(jnp.bfloat16)


def anywhere(count):
    return [pl.BlockSpec(memory_space=pl.ANY)] * count


def project(own, n, blocks, basis, turn):
    slots = blocks[0][0].shape[-2]
    depth, cols = basis.shape
    total = n * slots
    shape = (CAND, cols, total) if turn else (total, cols)
    steps = depth // KBLK
    return pl.pallas_call(
        functools.partial(project_kernel, n, shape_of(blocks), turn),
        out_shape=jax.ShapeDtypeStruct(shape, jnp.bfloat16),
        grid_spec=pltpu.PrefetchScalarGridSpec(
            num_scalar_prefetch=1,
            grid=(steps,),
            in_specs=anywhere(len(blocks) + 1),
            out_specs=pl.BlockSpec(shape, lambda k, own: (0,) * len(shape)),
            scratch_shapes=[pltpu.VMEM(x.shape, jnp.bfloat16) for x, _ in blocks] + [
                pltpu.VMEM((steps, KBLK, cols), jnp.bfloat16),
                pltpu.VMEM((total, KBLK), jnp.float32),
                pltpu.VMEM((total, cols), jnp.float32),
                pltpu.SemaphoreType.DMA((steps,)),
                pltpu.SemaphoreType.DMA((len(blocks),)),
            ],
        ),
        compiler_params=pltpu.CompilerParams(vmem_limit_bytes=VMEM),
        cost_estimate=pl.CostEstimate(flops=total, bytes_accessed=total, transcendentals=0),
    )(own, *[x for x, _ in blocks], basis)


def outer_kernel(blocks, own_ref, *refs):
    given = len(blocks)
    sources, left_any, eig_ref = refs[:given], refs[given], refs[given + 1]
    out_ref, *pieces = refs[-9 - given:-8]
    left, right, eig, out, eig_sems, out_sems, piece_sems, left_sem = refs[-8:]
    listed = flat(pieces, blocks)
    count = len(listed)
    step = pl.program_id(0)
    rows, cols = eig.shape[1:]
    depth = out.shape[0]

    def columns(s):
        m = jnp.int32(listed[0][2])
        for k in range(1, count):
            m = jnp.where(s == k, listed[k][2], m)
        return pl.ds(pl.multiple_of(jnp.bitwise_xor(m, own_ref[0]) * cols, cols), cols)

    def read(s):
        return pltpu.make_async_copy(eig_ref.at[:, columns(s)], eig.at[s], eig_sems.at[s])

    def write(s, c):
        slot = lax.rem(s, depth)
        return pltpu.make_async_copy(
            out.at[slot, c], out_ref.at[c, :, columns(s)], out_sems.at[slot, c]
        )

    @pl.when(step == 0)
    def _():
        copies = [pltpu.make_async_copy(left_any, left, left_sem)] + [
            pltpu.make_async_copy(source, piece, piece_sems.at[k])
            for k, (source, piece) in enumerate(zip(sources, pieces))
        ]
        for s in range(count):
            read(s).start()
            if s == 0:
                for copy in copies:
                    copy.start()
        for copy in copies:
            copy.wait()

    for k, (piece, e, _) in enumerate(listed):
        @pl.when(step == k)
        def _(piece=piece, e=e):
            right[...] = piece[...] if e is None else piece[e]

    read(step).wait()
    slot = lax.rem(step, depth)
    for c in range(CAND):
        @pl.when(step >= depth)
        def _(c=c):
            write(step - depth, c).wait()

    for r in range(0, rows, RBLK):
        shifted = eig[step, r:r + RBLK, :].astype(jnp.float32) + 0.01
        near = pl.reciprocal(shifted, approx=True)
        scale = near * (2.0 - shifted * near)
        for c in range(CAND):
            summed = jnp.dot(
                left[c, r:r + RBLK, :], right[...], preferred_element_type=jnp.float32
            )
            out[slot, c, r:r + RBLK, :] = (summed * scale).astype(jnp.bfloat16)
    for c in range(CAND):
        write(step, c).start()

    @pl.when(step == count - 1)
    def _():
        for s in range(max(0, count - depth), count):
            for c in range(CAND):
                write(s, c).wait()


def outer(own, blocks, left, eigvals, before):
    total, cols = blocks[0][0].shape[-2:]
    rows, width = eigvals.shape
    count = sum(len(entries) for _, entries in blocks)
    operands = [own] + [x for x, _ in blocks] + [left, eigvals]
    aliases = {}
    if before is not None:
        aliases = {len(operands): 0}
        operands.append(before)
    share = count * cols
    return pl.pallas_call(
        functools.partial(outer_kernel, shape_of(blocks)),
        out_shape=jax.ShapeDtypeStruct((CAND, rows, width), jnp.bfloat16),
        grid_spec=pltpu.PrefetchScalarGridSpec(
            num_scalar_prefetch=1,
            grid=(count,),
            in_specs=anywhere(len(operands) - 1),
            out_specs=pl.BlockSpec(memory_space=pl.ANY),
            scratch_shapes=[pltpu.VMEM(x.shape, jnp.bfloat16) for x, _ in blocks] + [
                pltpu.VMEM(left.shape, jnp.bfloat16),
                pltpu.VMEM((total, cols), jnp.bfloat16),
                pltpu.VMEM((count, rows, cols), jnp.bfloat16),
                pltpu.VMEM((FLIGHT, CAND, rows, cols), jnp.bfloat16),
                pltpu.SemaphoreType.DMA((count,)),
                pltpu.SemaphoreType.DMA((FLIGHT, CAND)),
                pltpu.SemaphoreType.DMA((len(blocks),)),
                pltpu.SemaphoreType.DMA(()),
            ],
        ),
        input_output_aliases=aliases,
        compiler_params=pltpu.CompilerParams(vmem_limit_bytes=VMEM),
        cost_estimate=pl.CostEstimate(
            flops=2 * total * rows * share,
            bytes_accessed=2 * rows * share * (CAND + 1),
            transcendentals=rows * share,
        ),
    )(*operands)


def by_swaps(factors_in, factors_out, basis_in, basis_out, eigvals, live_counts):
    n = lax.axis_size("dp")
    own = lax.axis_index("dp").astype(jnp.int32)[None]
    slots = factors_in.shape[0]
    column = (0, 4, 8, 12)
    pair = (2, 6, 10, 14)
    core = (1, 5, 9, 13)
    other = (3, 7, 11, 15)
    tie = lax.optimization_barrier

    a1, ap, a2, a3 = [swap(factors_in, m) for m in (4, 2, 8, 12)]
    keep = (lax.iota(jnp.int32, slots) < live_counts[0])[:, None]
    a, b = tie(tuple(
        jnp.where(keep, x, jnp.zeros_like(x)) for x in (factors_in, factors_out)
    ))
    a1, ap = tie((a1, ap))
    ap1 = swap(a1, 2)
    ap23 = swap(jnp.stack([a2, a3]), 2)
    a_column = jnp.stack([a, a1, a2, a3])
    a_core = swap(a_column, 1)
    b = after(b, a1, a2, a3, ap)
    b1, bp, b2, b3 = [swap(b, m) for m in (4, 2, 8, 12)]
    ap23, b1 = tie((ap23, b1))
    a_pair = jnp.stack([ap, ap1, ap23[0], ap23[1]])
    a_other = swap(a_pair, 1)
    pin = project(
        own, n, [(a_column, column), (a_pair, pair), (a_core, core), (a_other, other)],
        basis_in, False,
    )

    b1, b2, b3, bp = tie((b1, b2, b3, bp, pin))[:4]
    b_column = jnp.stack([b, b1, b2, b3])
    bp123 = swap(b_column[1:], 2)
    b_core = swap(b_column, 1)
    g1, gp, g2, g3 = [swap(pin, m) for m in (4, 2, 8, 12)]
    bp123, g1, g2, g3 = tie((bp123, g1, g2, g3))
    b_pair = jnp.concatenate([bp[None], bp123])
    b_other = swap(b_pair, 1)
    left = project(
        own, n, [(b_column, column), (b_pair, pair), (b_core, core), (b_other, other)],
        basis_out, True,
    )
    g1, g2, g3, gp = tie((g1, g2, g3, gp, left))[:4]
    g_column = jnp.stack([pin, g1, g2, g3])
    gp123 = swap(g_column[1:], 2)
    g_core = swap(g_column, 1)
    out = outer(own, [(g_column, column), (gp, [2])], left, eigvals, None)
    g_other = swap(jnp.concatenate([gp[None], after(gp123, out)]), 1)
    return outer(own, [(g_core, core), (gp123, pair[1:]), (g_other, other)], left, eigvals, out)


def solution(mesh):
    placed = (
        P(("groups", "dp"), "basis"),
        P(("groups", "dp"), "basis"),
        P("basis", "dp"),
        P("basis", "dp"),
        P("dp", None),
        P(("groups", "dp")),
    )
    chosen = by_swaps if mesh.shape["basis"] == 1 and mesh.shape["dp"] == 16 else general
    return jax.shard_map(
        chosen,
        mesh=mesh,
        in_specs=placed,
        out_specs=P(("groups", "basis"), "dp", None),
        check_vma=False,
    )
```

```python
import functools

import jax
import jax.numpy as jnp
from jax import lax
from jax.experimental import pallas as pl
from jax.experimental.pallas import tpu as pltpu
from jax.sharding import PartitionSpec as P

CAND = 4
KBLK = 1024
RBLK = 256
FLIGHT = 3
VMEM = 50 << 20


def general(factors_in, factors_out, basis_in, basis_out, eigvals, live_counts):
    slot_rows = factors_in.shape[0]
    keep = (lax.iota(jnp.int32, slot_rows) < live_counts[0])[:, None]
    masked = jnp.where(keep, factors_in, jnp.zeros_like(factors_in))
    partial_in = jnp.dot(
        lax.all_gather(masked, "dp", axis=0, tiled=True),
        basis_in,
        preferred_element_type=jnp.float32,
    )
    partial_out = jnp.dot(
        lax.all_gather(factors_out, "dp", axis=0, tiled=True),
        basis_out,
        preferred_element_type=jnp.float32,
    )
    halves = lax.axis_size("basis")
    share = partial_in.shape[0] // halves
    summed_in, summed_out = lax.psum((partial_in, partial_out), "basis")
    first = lax.axis_index("basis") * share
    proj_in = lax.dynamic_slice_in_dim(summed_in, first, share, 0).astype(jnp.bfloat16)
    proj_out = lax.dynamic_slice_in_dim(summed_out, first, share, 0).astype(jnp.bfloat16)
    cand_local = CAND // halves
    per_cand = share // cand_local
    pout_grouped = proj_out.reshape(cand_local, per_cand, proj_out.shape[1])
    shifted = eigvals.astype(jnp.float32) + 0.01
    piece = lax.all_gather(proj_in, "dp", axis=1, tiled=True)
    pin_grouped = piece.reshape(cand_local, per_cand, piece.shape[1])
    summed = jnp.einsum(
        "ati,atj->aij", pout_grouped, pin_grouped, preferred_element_type=jnp.float32
    )
    return (summed / shifted[None, :, :]).astype(jnp.bfloat16)


def swap(x, m):
    n = lax.axis_size("dp")
    return lax.ppermute(x, "dp", [(d, d ^ m) for d in range(n)])


def after(x, *others):
    return lax.optimization_barrier((x,) + others)[0]


def project_kernel(blocks, turn, own_ref, *refs):
    count = len(blocks)
    sources, basis_ref, out_ref = refs[:count], refs[count], refs[count + 1]
    pieces, (held, rows, sems, piece_sems) = refs[count + 2:-4], refs[-4:]
    chunks, width = held.shape[:2]
    slots = pieces[0].shape[-2]
    copies = [
        pltpu.make_async_copy(source, piece, piece_sems.at[k])
        for k, (source, piece) in enumerate(zip(sources, pieces))
    ]
    reads = [
        pltpu.make_async_copy(basis_ref.at[pl.ds(k * width, width)], held.at[k], sems.at[k])
        for k in range(chunks)
    ]
    reads[0].start()
    for copy in copies:
        copy.start()
    for read in reads[1:]:
        read.start()
    for copy, piece, entries in zip(copies, pieces, blocks):
        copy.wait()
        for e, m in enumerate(entries):
            rows[m * slots:(m + 1) * slots, :] = piece[e].astype(jnp.float32)
    acc = None
    for k in range(chunks):
        reads[k].wait()
        part = jnp.dot(
            rows[:, k * width:(k + 1) * width].astype(jnp.bfloat16),
            held[k],
            preferred_element_type=jnp.float32,
        )
        acc = part if acc is None else acc + part
    total = rows.shape[0]
    to = lax.broadcasted_iota(jnp.int32, (total, total), 0)
    come = lax.broadcasted_iota(jnp.int32, (total, total), 1)
    where = jnp.bitwise_xor(come // slots, own_ref[0]) * slots + come % slots
    pick = jnp.where(to == where, 1.0, 0.0).astype(jnp.bfloat16)
    proj = jnp.dot(pick, acc.astype(jnp.bfloat16), preferred_element_type=jnp.float32)
    if turn:
        turned = proj.T
        token = lax.broadcasted_iota(jnp.int32, turned.shape, 1)
        for c in range(CAND):
            own_tokens = token // (total // CAND) == c
            out_ref[c] = jnp.where(own_tokens, turned, 0.0).astype(jnp.bfloat16)
    else:
        out_ref[...] = proj.astype(jnp.bfloat16)


def anywhere(count):
    return [pl.BlockSpec(memory_space=pl.ANY)] * count


def project(own, blocks, basis, turn):
    slots = blocks[0][0].shape[-2]
    depth, cols = basis.shape
    total = slots * sum(len(entries) for _, entries in blocks)
    shape = (CAND, cols, total) if turn else (total, cols)
    chunks = depth // KBLK
    return pl.pallas_call(
        functools.partial(project_kernel, [entries for _, entries in blocks], turn),
        out_shape=jax.ShapeDtypeStruct(shape, jnp.bfloat16),
        in_specs=[pl.BlockSpec(memory_space=pltpu.SMEM)] + anywhere(len(blocks) + 1),
        out_specs=pl.BlockSpec(memory_space=pltpu.VMEM),
        scratch_shapes=[pltpu.VMEM(x.shape, jnp.bfloat16) for x, _ in blocks] + [
            pltpu.VMEM((chunks, KBLK, cols), jnp.bfloat16),
            pltpu.VMEM((total, depth), jnp.float32),
            pltpu.SemaphoreType.DMA((chunks,)),
            pltpu.SemaphoreType.DMA((len(blocks),)),
        ],
        compiler_params=pltpu.CompilerParams(vmem_limit_bytes=VMEM),
        cost_estimate=pl.CostEstimate(flops=total, bytes_accessed=total, transcendentals=0),
    )(own, *[x for x, _ in blocks], basis)


def outer_kernel(blocks, own_ref, *refs):
    given = len(blocks)
    sources, left_any, eig_ref = refs[:given], refs[given], refs[given + 1]
    out_ref, left, right, eig, scale, out, eig_sems, out_sems, piece_sems, left_sem = refs[-10:]
    order = [m for entries in blocks for m in entries]
    count = len(order)
    rows, cols = eig.shape[1:]
    depth = out.shape[0]

    def columns(s):
        m = jnp.int32(order[0])
        for k in range(1, count):
            m = jnp.where(s == k, order[k], m)
        return pl.ds(pl.multiple_of(jnp.bitwise_xor(m, own_ref[0]) * cols, cols), cols)

    def read(s):
        return pltpu.make_async_copy(eig_ref.at[:, columns(s)], eig.at[s], eig_sems.at[s])

    def write(s, c):
        slot = lax.rem(s, depth)
        return pltpu.make_async_copy(
            out.at[slot, c], out_ref.at[c, :, columns(s)], out_sems.at[slot, c]
        )

    copies, at = [pltpu.make_async_copy(left_any, left, left_sem)], 0
    for k, (source, entries) in enumerate(zip(sources, blocks)):
        room = right.at[pl.ds(at, len(entries))]
        copies.append(pltpu.make_async_copy(source, room, piece_sems.at[k]))
        at += len(entries)
    read(0).start()
    for copy in copies:
        copy.start()
    for s in range(1, count):
        read(s).start()
    for copy in copies:
        copy.wait()

    @pl.loop(0, count)
    def _(s):
        slot = lax.rem(s, depth)
        read(s).wait()
        shifted = eig[s].astype(jnp.float32) + 0.01
        near = pl.reciprocal(shifted, approx=True)
        scale[...] = near * (2.0 - shifted * near)
        for c in range(CAND):
            @pl.when(s >= depth)
            def _():
                write(s - depth, c).wait()

            for r in range(0, rows, RBLK):
                summed = jnp.dot(
                    left[c, r:r + RBLK, :], right[s], preferred_element_type=jnp.float32
                )
                out[slot, c, r:r + RBLK, :] = (summed * scale[r:r + RBLK, :]).astype(jnp.bfloat16)
            write(s, c).start()

    for s in range(max(0, count - depth), count):
        for c in range(CAND):
            write(s, c).wait()


def outer(own, blocks, left, eigvals, before):
    total, cols = blocks[0][0].shape[-2:]
    rows, width = eigvals.shape
    count = sum(len(entries) for _, entries in blocks)
    operands = [own] + [x for x, _ in blocks] + [left, eigvals]
    aliases = {}
    if before is not None:
        aliases = {len(operands): 0}
        operands.append(before)
    share = count * cols
    return pl.pallas_call(
        functools.partial(outer_kernel, [entries for _, entries in blocks]),
        out_shape=jax.ShapeDtypeStruct((CAND, rows, width), jnp.bfloat16),
        in_specs=[pl.BlockSpec(memory_space=pltpu.SMEM)] + anywhere(len(operands) - 1),
        out_specs=pl.BlockSpec(memory_space=pl.ANY),
        scratch_shapes=[
            pltpu.VMEM(left.shape, jnp.bfloat16),
            pltpu.VMEM((count, total, cols), jnp.bfloat16),
            pltpu.VMEM((count, rows, cols), jnp.bfloat16),
            pltpu.VMEM((rows, cols), jnp.float32),
            pltpu.VMEM((FLIGHT, CAND, rows, cols), jnp.bfloat16),
            pltpu.SemaphoreType.DMA((count,)),
            pltpu.SemaphoreType.DMA((FLIGHT, CAND)),
            pltpu.SemaphoreType.DMA((len(blocks),)),
            pltpu.SemaphoreType.DMA(()),
        ],
        input_output_aliases=aliases,
        compiler_params=pltpu.CompilerParams(vmem_limit_bytes=VMEM),
        cost_estimate=pl.CostEstimate(
            flops=2 * total * rows * share,
            bytes_accessed=2 * rows * share * (CAND + 1),
            transcendentals=rows * share,
        ),
    )(*operands)


def by_swaps(factors_in, factors_out, basis_in, basis_out, eigvals, live_counts):
    own = lax.axis_index("dp").astype(jnp.int32)[None]
    slots = factors_in.shape[0]
    column = (0, 4, 8, 12)
    pair = (2, 6, 10, 14)
    core = (1, 5, 9, 13)
    other = (3, 7, 11, 15)
    tie = lax.optimization_barrier

    a1, ap, a2, a3 = [swap(factors_in, m) for m in (4, 2, 8, 12)]
    keep = (lax.iota(jnp.int32, slots) < live_counts[0])[:, None]
    a, b = tie(tuple(
        jnp.where(keep, x, jnp.zeros_like(x)) for x in (factors_in, factors_out)
    ))
    a1, ap = tie((a1, ap))
    ap1 = swap(a1, 2)
    ap23 = swap(jnp.stack([a2, a3]), 2)
    a_column = jnp.stack([a, a1, a2, a3])
    a_core = swap(a_column, 1)
    b = after(b, a_column)
    b1, bp, b2, b3 = [swap(b, m) for m in (4, 2, 8, 12)]
    ap23, b1 = tie((ap23, b1))
    a_pair = jnp.stack([ap, ap1, ap23[0], ap23[1]])
    a_other = swap(a_pair, 1)
    pin = project(
        own, [(a_column, column), (a_pair, pair), (a_core, core), (a_other, other)],
        basis_in, False,
    )

    b1, b2, b3, bp = tie((b1, b2, b3, bp, pin))[:4]
    bp123 = swap(jnp.stack([b1, b2, b3]), 2)
    b_column = jnp.stack([b, b1, b2, b3])
    b_core = swap(b_column, 1)
    sent, b_column = tie((pin, b_column))
    g1, gp, g2, g3 = [swap(sent, m) for m in (4, 2, 8, 12)]
    bp123, g1, g2, g3 = tie((bp123, g1, g2, g3))
    b_pair = jnp.concatenate([bp[None], bp123])
    b_other = swap(b_pair, 1)
    g_column = jnp.stack([pin, g1, g2, g3])
    gp123 = swap(jnp.stack([g1, g2, g3]), 2)
    g_core = swap(g_column, 1)
    b_other, g_column = tie((b_other, g_column))
    left = project(
        own, [(b_column, column), (b_pair, pair), (b_core, core), (b_other, other)],
        basis_out, True,
    )
    out = outer(own, [(g_column, column), (gp[None], pair[:1])], left, eigvals, None)
    g_other = swap(jnp.concatenate([gp[None], after(gp123, out)]), 1)
    return outer(own, [(g_core, core), (gp123, pair[1:]), (g_other, other)], left, eigvals, out)


def solution(mesh):
    placed = (
        P(("groups", "dp"), "basis"),
        P(("groups", "dp"), "basis"),
        P("basis", "dp"),
        P("basis", "dp"),
        P("dp", None),
        P(("groups", "dp")),
    )
    chosen = by_swaps if mesh.shape["basis"] == 1 and mesh.shape["dp"] == 16 else general
    return jax.shard_map(
        chosen,
        mesh=mesh,
        in_specs=placed,
        out_specs=P(("groups", "basis"), "dp", None),
        check_vma=False,
    )
```

```python
import functools

import jax
import jax.numpy as jnp
from jax import lax
from jax.experimental import pallas as pl
from jax.experimental.pallas import tpu as pltpu
from jax.sharding import PartitionSpec as P

CAND = 4
KBLK = 1024
RBLK = 256
FLIGHT = 3
VMEM = 50 << 20


def general(factors_in, factors_out, basis_in, basis_out, eigvals, live_counts):
    slot_rows = factors_in.shape[0]
    keep = (lax.iota(jnp.int32, slot_rows) < live_counts[0])[:, None]
    masked = jnp.where(keep, factors_in, jnp.zeros_like(factors_in))
    partial_in = jnp.dot(
        lax.all_gather(masked, "dp", axis=0, tiled=True),
        basis_in,
        preferred_element_type=jnp.float32,
    )
    partial_out = jnp.dot(
        lax.all_gather(factors_out, "dp", axis=0, tiled=True),
        basis_out,
        preferred_element_type=jnp.float32,
    )
    halves = lax.axis_size("basis")
    share = partial_in.shape[0] // halves
    summed_in, summed_out = lax.psum((partial_in, partial_out), "basis")
    first = lax.axis_index("basis") * share
    proj_in = lax.dynamic_slice_in_dim(summed_in, first, share, 0).astype(jnp.bfloat16)
    proj_out = lax.dynamic_slice_in_dim(summed_out, first, share, 0).astype(jnp.bfloat16)
    cand_local = CAND // halves
    per_cand = share // cand_local
    pout_grouped = proj_out.reshape(cand_local, per_cand, proj_out.shape[1])
    shifted = eigvals.astype(jnp.float32) + 0.01
    piece = lax.all_gather(proj_in, "dp", axis=1, tiled=True)
    pin_grouped = piece.reshape(cand_local, per_cand, piece.shape[1])
    summed = jnp.einsum(
        "ati,atj->aij", pout_grouped, pin_grouped, preferred_element_type=jnp.float32
    )
    return (summed / shifted[None, :, :]).astype(jnp.bfloat16)


def swap(x, m):
    n = lax.axis_size("dp")
    return lax.ppermute(x, "dp", [(d, d ^ m) for d in range(n)])


def after(x, *others):
    return lax.optimization_barrier((x,) + others)[0]


def project_kernel(blocks, which, turn, own_ref, *refs):
    count = len(blocks)
    sources, basis_ref, out_ref = refs[:count], refs[count], refs[count + 1]
    pieces, (held, rows, sems, piece_sems) = refs[count + 2:-4], refs[-4:]
    chunks, width = held.shape[:2]
    slots = pieces[0].shape[-2]
    copies = [
        pltpu.make_async_copy(source.at[:, which], piece, piece_sems.at[k])
        for k, (source, piece) in enumerate(zip(sources, pieces))
    ]
    reads = [
        pltpu.make_async_copy(basis_ref.at[pl.ds(k * width, width)], held.at[k], sems.at[k])
        for k in range(chunks)
    ]
    reads[0].start()
    for copy in copies:
        copy.start()
    for read in reads[1:]:
        read.start()
    for copy, piece, entries in zip(copies, pieces, blocks):
        copy.wait()
        for e, m in enumerate(entries):
            rows[m * slots:(m + 1) * slots, :] = piece[e].astype(jnp.float32)
    acc = None
    for k in range(chunks):
        reads[k].wait()
        part = jnp.dot(
            rows[:, k * width:(k + 1) * width].astype(jnp.bfloat16),
            held[k],
            preferred_element_type=jnp.float32,
        )
        acc = part if acc is None else acc + part
    total = rows.shape[0]
    to = lax.broadcasted_iota(jnp.int32, (total, total), 0)
    come = lax.broadcasted_iota(jnp.int32, (total, total), 1)
    where = jnp.bitwise_xor(come // slots, own_ref[0]) * slots + come % slots
    pick = jnp.where(to == where, 1.0, 0.0).astype(jnp.bfloat16)
    proj = jnp.dot(pick, acc.astype(jnp.bfloat16), preferred_element_type=jnp.float32)
    if turn:
        turned = proj.T
        token = lax.broadcasted_iota(jnp.int32, turned.shape, 1)
        for c in range(CAND):
            own_tokens = token // (total // CAND) == c
            out_ref[c] = jnp.where(own_tokens, turned, 0.0).astype(jnp.bfloat16)
    else:
        out_ref[...] = proj.astype(jnp.bfloat16)


def anywhere(count):
    return [pl.BlockSpec(memory_space=pl.ANY)] * count


def project(own, blocks, basis, which, turn):
    slots = blocks[0][0].shape[-2]
    depth, cols = basis.shape
    total = slots * sum(len(entries) for _, entries in blocks)
    shape = (CAND, cols, total) if turn else (total, cols)
    chunks = depth // KBLK
    return pl.pallas_call(
        functools.partial(project_kernel, [entries for _, entries in blocks], which, turn),
        out_shape=jax.ShapeDtypeStruct(shape, jnp.bfloat16),
        in_specs=[pl.BlockSpec(memory_space=pltpu.SMEM)] + anywhere(len(blocks) + 1),
        out_specs=pl.BlockSpec(memory_space=pltpu.VMEM),
        scratch_shapes=[
            pltpu.VMEM((len(entries), slots, depth), jnp.bfloat16) for _, entries in blocks
        ] + [
            pltpu.VMEM((chunks, KBLK, cols), jnp.bfloat16),
            pltpu.VMEM((total, depth), jnp.float32),
            pltpu.SemaphoreType.DMA((chunks,)),
            pltpu.SemaphoreType.DMA((len(blocks),)),
        ],
        compiler_params=pltpu.CompilerParams(vmem_limit_bytes=VMEM),
        cost_estimate=pl.CostEstimate(flops=total, bytes_accessed=total, transcendentals=0),
    )(own, *[x for x, _ in blocks], basis)


def outer_kernel(blocks, own_ref, *refs):
    given = len(blocks)
    sources, left_any, eig_ref = refs[:given], refs[given], refs[given + 1]
    out_ref, left, right, eig, out, eig_sems, out_sems, piece_sems, left_sem = refs[-9:]
    order = [m for entries in blocks for m in entries]
    count = len(order)
    rows, cols = eig.shape[1:]
    depth = out.shape[0]

    def columns(s):
        m = jnp.int32(order[0])
        for k in range(1, count):
            m = jnp.where(s == k, order[k], m)
        return pl.ds(pl.multiple_of(jnp.bitwise_xor(m, own_ref[0]) * cols, cols), cols)

    def read(s):
        return pltpu.make_async_copy(eig_ref.at[:, columns(s)], eig.at[s], eig_sems.at[s])

    def write(s, c):
        slot = lax.rem(s, depth)
        return pltpu.make_async_copy(
            out.at[slot, c], out_ref.at[c, :, columns(s)], out_sems.at[slot, c]
        )

    copies, at = [pltpu.make_async_copy(left_any, left, left_sem)], 0
    for k, (source, entries) in enumerate(zip(sources, blocks)):
        room = right.at[pl.ds(at, len(entries))]
        copies.append(pltpu.make_async_copy(source, room, piece_sems.at[k]))
        at += len(entries)
    read(0).start()
    for copy in copies:
        copy.start()
    for s in range(1, count):
        read(s).start()
    for copy in copies:
        copy.wait()

    def work(s, slot):
        read(s).wait()
        for r in range(0, rows, RBLK):
            shifted = eig[s, r:r + RBLK, :].astype(jnp.float32) + 0.01
            near = pl.reciprocal(shifted, approx=True)
            scale = near * (2.0 - shifted * near)
            for c in range(CAND):
                summed = jnp.dot(
                    left[c, r:r + RBLK, :], right[s], preferred_element_type=jnp.float32
                )
                out[slot, c, r:r + RBLK, :] = (summed * scale).astype(jnp.bfloat16)
        for c in range(CAND):
            write(s, c).start()

    for s in range(depth):
        work(s, s)

    @pl.loop(depth, count)
    def _(s):
        for c in range(CAND):
            write(s - depth, c).wait()
        work(s, lax.rem(s, depth))

    for s in range(max(0, count - depth), count):
        for c in range(CAND):
            write(s, c).wait()


def outer(own, blocks, left, eigvals, before):
    total, cols = blocks[0][0].shape[-2:]
    rows, width = eigvals.shape
    count = sum(len(entries) for _, entries in blocks)
    operands = [own] + [x for x, _ in blocks] + [left, eigvals]
    aliases = {}
    if before is not None:
        aliases = {len(operands): 0}
        operands.append(before)
    share = count * cols
    return pl.pallas_call(
        functools.partial(outer_kernel, [entries for _, entries in blocks]),
        out_shape=jax.ShapeDtypeStruct((CAND, rows, width), jnp.bfloat16),
        in_specs=[pl.BlockSpec(memory_space=pltpu.SMEM)] + anywhere(len(operands) - 1),
        out_specs=pl.BlockSpec(memory_space=pl.ANY),
        scratch_shapes=[
            pltpu.VMEM(left.shape, jnp.bfloat16),
            pltpu.VMEM((count, total, cols), jnp.bfloat16),
            pltpu.VMEM((count, rows, cols), jnp.bfloat16),
            pltpu.VMEM((FLIGHT, CAND, rows, cols), jnp.bfloat16),
            pltpu.SemaphoreType.DMA((count,)),
            pltpu.SemaphoreType.DMA((FLIGHT, CAND)),
            pltpu.SemaphoreType.DMA((len(blocks),)),
            pltpu.SemaphoreType.DMA(()),
        ],
        input_output_aliases=aliases,
        compiler_params=pltpu.CompilerParams(vmem_limit_bytes=VMEM),
        cost_estimate=pl.CostEstimate(
            flops=2 * total * rows * share,
            bytes_accessed=2 * rows * share * (CAND + 1),
            transcendentals=rows * share,
        ),
    )(*operands)


def by_swaps(factors_in, factors_out, basis_in, basis_out, eigvals, live_counts):
    own = lax.axis_index("dp").astype(jnp.int32)[None]
    column = (0, 4, 8, 12)
    pair = (2, 6, 10, 14)
    core = (1, 5, 9, 13)
    other = (3, 7, 11, 15)
    tie = lax.optimization_barrier

    keep = (lax.iota(jnp.int32, factors_in.shape[0]) < live_counts[0])[:, None]
    f = jnp.stack([factors_in, jnp.where(keep, factors_out, jnp.zeros_like(factors_out))])
    f1, fp, f2, f3 = [swap(f, m) for m in (4, 2, 8, 12)]
    f1, fp = tie((f1, fp))
    fp1 = swap(f1, 2)
    f2, f3 = tie((f2, f3, fp1))[:2]
    fp23 = swap(jnp.stack([f2, f3]), 2)
    f_column = jnp.stack([f, f1, f2, f3])
    f_core = swap(f_column, 1)
    f_pair = jnp.stack([fp, fp1, fp23[0], fp23[1]])
    f_other = swap(f_pair, 1)
    blocks = [(f_column, column), (f_pair, pair), (f_core, core), (f_other, other)]
    pin = project(own, blocks, basis_in, 0, False)

    g1, gp, g2, g3 = [swap(pin, m) for m in (4, 2, 8, 12)]
    left = project(own, blocks, basis_out, 1, True)
    g1, g2, g3, gp = tie((g1, g2, g3, gp, left))[:4]
    g_column = jnp.stack([pin, g1, g2, g3])
    gp123 = swap(g_column[1:], 2)
    g_core = swap(g_column, 1)
    out = outer(own, [(g_column, column), (gp[None], pair[:1])], left, eigvals, None)
    g_other = swap(jnp.concatenate([gp[None], after(gp123, out)]), 1)
    return outer(own, [(g_core, core), (gp123, pair[1:]), (g_other, other)], left, eigvals, out)


def solution(mesh):
    placed = (
        P(("groups", "dp"), "basis"),
        P(("groups", "dp"), "basis"),
        P("basis", "dp"),
        P("basis", "dp"),
        P("dp", None),
        P(("groups", "dp")),
    )
    chosen = by_swaps if mesh.shape["basis"] == 1 and mesh.shape["dp"] == 16 else general
    return jax.shard_map(
        chosen,
        mesh=mesh,
        in_specs=placed,
        out_specs=P(("groups", "basis"), "dp", None),
        check_vma=False,
    )
```

```python
import functools

import jax
import jax.numpy as jnp
from jax import lax
from jax.experimental import pallas as pl
from jax.experimental.pallas import tpu as pltpu
from jax.sharding import PartitionSpec as P

CAND = 4
KBLK = 1024
RBLK = 256
FLIGHT = 3
VMEM = 20 << 20
PARTS = 4


def general(factors_in, factors_out, basis_in, basis_out, eigvals, live_counts):
    slot_rows = factors_in.shape[0]
    keep = (lax.iota(jnp.int32, slot_rows) < live_counts[0])[:, None]
    masked = jnp.where(keep, factors_in, jnp.zeros_like(factors_in))
    partial_in = jnp.dot(
        lax.all_gather(masked, "dp", axis=0, tiled=True),
        basis_in,
        preferred_element_type=jnp.float32,
    )
    partial_out = jnp.dot(
        lax.all_gather(factors_out, "dp", axis=0, tiled=True),
        basis_out,
        preferred_element_type=jnp.float32,
    )
    halves = lax.axis_size("basis")
    share = partial_in.shape[0] // halves
    summed_in, summed_out = lax.psum((partial_in, partial_out), "basis")
    first = lax.axis_index("basis") * share
    proj_in = lax.dynamic_slice_in_dim(summed_in, first, share, 0).astype(jnp.bfloat16)
    proj_out = lax.dynamic_slice_in_dim(summed_out, first, share, 0).astype(jnp.bfloat16)
    cand_local = CAND // halves
    per_cand = share // cand_local
    pout_grouped = proj_out.reshape(cand_local, per_cand, proj_out.shape[1])
    shifted = eigvals.astype(jnp.float32) + 0.01
    piece = lax.all_gather(proj_in, "dp", axis=1, tiled=True)
    pin_grouped = piece.reshape(cand_local, per_cand, piece.shape[1])
    summed = jnp.einsum(
        "ati,atj->aij", pout_grouped, pin_grouped, preferred_element_type=jnp.float32
    )
    return (summed / shifted[None, :, :]).astype(jnp.bfloat16)


def swap(x, m):
    n = lax.axis_size("dp")
    return lax.ppermute(x, "dp", [(d, d ^ m) for d in range(n)])


def after(x, *others):
    return lax.optimization_barrier((x,) + others)[0]


def project_kernel(blocks, which, turn, own_ref, *refs):
    count = len(blocks)
    sources, basis_ref, out_ref = refs[:count], refs[count], refs[count + 1]
    pieces, (held, rows, sems, piece_sems) = refs[count + 2:-4], refs[-4:]
    chunks, width = held.shape[:2]
    slots = pieces[0].shape[-2]
    copies = [
        pltpu.make_async_copy(source.at[:, which], piece, piece_sems.at[k])
        for k, (source, piece) in enumerate(zip(sources, pieces))
    ]
    reads = [
        pltpu.make_async_copy(basis_ref.at[pl.ds(k * width, width)], held.at[k], sems.at[k])
        for k in range(chunks)
    ]
    reads[0].start()
    for copy in copies:
        copy.start()
    for read in reads[1:]:
        read.start()
    for copy, piece, entries in zip(copies, pieces, blocks):
        copy.wait()
        for e, m in enumerate(entries):
            rows[m * slots:(m + 1) * slots, :] = piece[e].astype(jnp.float32)
    acc = None
    for k in range(chunks):
        reads[k].wait()
        part = jnp.dot(
            rows[:, k * width:(k + 1) * width].astype(jnp.bfloat16),
            held[k],
            preferred_element_type=jnp.float32,
        )
        acc = part if acc is None else acc + part
    total = rows.shape[0]
    to = lax.broadcasted_iota(jnp.int32, (total, total), 0)
    come = lax.broadcasted_iota(jnp.int32, (total, total), 1)
    where = jnp.bitwise_xor(come // slots, own_ref[0]) * slots + come % slots
    pick = jnp.where(to == where, 1.0, 0.0).astype(jnp.bfloat16)
    proj = jnp.dot(pick, acc.astype(jnp.bfloat16), preferred_element_type=jnp.float32)
    if turn:
        turned = proj.T
        token = lax.broadcasted_iota(jnp.int32, turned.shape, 1)
        for c in range(CAND):
            own_tokens = token // (total // CAND) == c
            out_ref[c] = jnp.where(own_tokens, turned, 0.0).astype(jnp.bfloat16)
    else:
        out_ref[...] = proj.astype(jnp.bfloat16)


def anywhere(count):
    return [pl.BlockSpec(memory_space=pl.ANY)] * count


def project(own, blocks, basis, which, turn):
    slots = blocks[0][0].shape[-2]
    depth, cols = basis.shape
    total = slots * sum(len(entries) for _, entries in blocks)
    shape = (CAND, cols, total) if turn else (total, cols)
    chunks = depth // KBLK
    return pl.pallas_call(
        functools.partial(project_kernel, [entries for _, entries in blocks], which, turn),
        out_shape=jax.ShapeDtypeStruct(shape, jnp.bfloat16),
        in_specs=[pl.BlockSpec(memory_space=pltpu.SMEM)] + anywhere(len(blocks) + 1),
        out_specs=pl.BlockSpec(memory_space=pltpu.VMEM),
        scratch_shapes=[
            pltpu.VMEM((len(entries), slots, depth), jnp.bfloat16) for _, entries in blocks
        ] + [
            pltpu.VMEM((chunks, KBLK, cols), jnp.bfloat16),
            pltpu.VMEM((total, depth), jnp.float32),
            pltpu.SemaphoreType.DMA((chunks,)),
            pltpu.SemaphoreType.DMA((len(blocks),)),
        ],
        compiler_params=pltpu.CompilerParams(vmem_limit_bytes=VMEM),
        cost_estimate=pl.CostEstimate(flops=total, bytes_accessed=total, transcendentals=0),
    )(own, *[x for x, _ in blocks], basis)


def outer_kernel(blocks, own_ref, *refs):
    given = len(blocks)
    sources, left_any, eig_ref = refs[:given], refs[given], refs[given + 1]
    out_ref, left, right, eig, out, eig_sems, out_sems, piece_sems, left_sem = refs[-9:]
    order = [m for entries in blocks for m in entries]
    count = len(order)
    rows, cols = eig.shape[1:]
    depth = out.shape[0]

    def columns(s):
        m = jnp.int32(order[0])
        for k in range(1, count):
            m = jnp.where(s == k, order[k], m)
        return pl.ds(pl.multiple_of(jnp.bitwise_xor(m, own_ref[0]) * cols, cols), cols)

    def read(s):
        return pltpu.make_async_copy(eig_ref.at[:, columns(s)], eig.at[s], eig_sems.at[s])

    def write(s, c):
        slot = lax.rem(s, depth)
        return pltpu.make_async_copy(
            out.at[slot, c], out_ref.at[c, :, columns(s)], out_sems.at[slot, c]
        )

    copies, at = [pltpu.make_async_copy(left_any, left, left_sem)], 0
    for k, (source, entries) in enumerate(zip(sources, blocks)):
        room = right.at[pl.ds(at, len(entries))]
        copies.append(pltpu.make_async_copy(source, room, piece_sems.at[k]))
        at += len(entries)
    read(0).start()
    for copy in copies:
        copy.start()
    for s in range(1, count):
        read(s).start()
    for copy in copies:
        copy.wait()

    def work(s, slot):
        read(s).wait()
        for r in range(0, rows, RBLK):
            shifted = eig[s, r:r + RBLK, :].astype(jnp.float32) + 0.01
            near = pl.reciprocal(shifted, approx=True)
            scale = near * (2.0 - shifted * near)
            for c in range(CAND):
                summed = jnp.dot(
                    left[c, r:r + RBLK, :], right[s], preferred_element_type=jnp.float32
                )
                out[slot, c, r:r + RBLK, :] = (summed * scale).astype(jnp.bfloat16)
        for c in range(CAND):
            write(s, c).start()

    for s in range(depth):
        work(s, s)

    @pl.loop(depth, count)
    def _(s):
        for c in range(CAND):
            write(s - depth, c).wait()
        work(s, lax.rem(s, depth))

    for s in range(max(0, count - depth), count):
        for c in range(CAND):
            write(s, c).wait()


def outer(own, blocks, left, eigvals, before):
    total, cols = blocks[0][0].shape[-2:]
    rows, width = eigvals.shape
    count = sum(len(entries) for _, entries in blocks)
    operands = [own] + [x for x, _ in blocks] + [left, eigvals]
    aliases = {}
    if before is not None:
        aliases = {len(operands): 0}
        operands.append(before)
    share = count * cols
    return pl.pallas_call(
        functools.partial(outer_kernel, [entries for _, entries in blocks]),
        out_shape=jax.ShapeDtypeStruct((CAND, rows, width), jnp.bfloat16),
        in_specs=[pl.BlockSpec(memory_space=pltpu.SMEM)] + anywhere(len(operands) - 1),
        out_specs=pl.BlockSpec(memory_space=pl.ANY),
        scratch_shapes=[
            pltpu.VMEM(left.shape, jnp.bfloat16),
            pltpu.VMEM((count, total, cols), jnp.bfloat16),
            pltpu.VMEM((count, rows, cols), jnp.bfloat16),
            pltpu.VMEM((FLIGHT, CAND, rows, cols), jnp.bfloat16),
            pltpu.SemaphoreType.DMA((count,)),
            pltpu.SemaphoreType.DMA((FLIGHT, CAND)),
            pltpu.SemaphoreType.DMA((len(blocks),)),
            pltpu.SemaphoreType.DMA(()),
        ],
        input_output_aliases=aliases,
        compiler_params=pltpu.CompilerParams(vmem_limit_bytes=VMEM),
        cost_estimate=pl.CostEstimate(
            flops=2 * total * rows * share,
            bytes_accessed=2 * rows * share * (CAND + 1),
            transcendentals=rows * share,
        ),
    )(*operands)


def stage_kernel(count, *refs):
    sources, (ready_ref, *kept), sems = refs[:count], refs[count:-1], refs[-1]
    copies = []
    for k, (source, keep) in enumerate(zip(sources, kept)):
        part = source.shape[0] // PARTS
        for p in range(PARTS):
            rows = pl.ds(p * part, part)
            copies.append(pltpu.make_async_copy(source.at[rows], keep.at[rows], sems.at[k, p]))
    for copy in copies:
        copy.start()
    for copy in copies:
        copy.wait()


def stage(arrays, ready):
    return pl.pallas_call(
        functools.partial(stage_kernel, len(arrays)),
        out_shape=[pltpu.VMEM(x.shape, x.dtype) for x in arrays],
        in_specs=anywhere(len(arrays) + 1),
        out_specs=anywhere(len(arrays)),
        scratch_shapes=[pltpu.SemaphoreType.DMA((len(arrays), PARTS))],
        compiler_params=pltpu.CompilerParams(vmem_limit_bytes=1 << 20),
        cost_estimate=pl.CostEstimate(flops=1, bytes_accessed=1, transcendentals=0),
    )(*[pltpu.with_memory_space_constraint(x, pltpu.HBM) for x in arrays], ready)


def by_swaps(factors_in, factors_out, basis_in, basis_out, eigvals, live_counts):
    own = lax.axis_index("dp").astype(jnp.int32)[None]
    column = (0, 4, 8, 12)
    pair = (2, 6, 10, 14)
    core = (1, 5, 9, 13)
    other = (3, 7, 11, 15)
    tie = lax.optimization_barrier

    keep = (lax.iota(jnp.int32, factors_in.shape[0]) < live_counts[0])[:, None]
    f = jnp.stack([factors_in, jnp.where(keep, factors_out, jnp.zeros_like(factors_out))])
    f1, fp, f2, f3 = [swap(f, m) for m in (4, 2, 8, 12)]
    f1, fp = tie((f1, fp))
    fp1 = swap(f1, 2)
    basis_in, basis_out = stage([basis_in, basis_out], f1)
    f2, f3 = tie((f2, f3, fp1, basis_in, basis_out))[:2]
    fp23 = swap(jnp.stack([f2, f3]), 2)
    f_column = jnp.stack([f, f1, f2, f3])
    f_core = swap(f_column, 1)
    eigvals, = stage([eigvals], f_column)
    fp23, eigvals = tie((fp23, eigvals))
    f_pair = jnp.stack([fp, fp1, fp23[0], fp23[1]])
    f_other = swap(f_pair, 1)
    blocks = [(f_column, column), (f_pair, pair), (f_core, core), (f_other, other)]
    pin = project(own, blocks, basis_in, 0, False)

    g1, gp, g2, g3 = [swap(pin, m) for m in (4, 2, 8, 12)]
    left = project(own, blocks, basis_out, 1, True)
    g1, g2, g3, gp = tie((g1, g2, g3, gp, left))[:4]
    g_column = jnp.stack([pin, g1, g2, g3])
    gp123 = swap(g_column[1:], 2)
    g_core = swap(g_column, 1)
    out = outer(own, [(g_column, column), (gp[None], pair[:1])], left, eigvals, None)
    g_other = swap(jnp.concatenate([gp[None], after(gp123, out)]), 1)
    return outer(own, [(g_core, core), (gp123, pair[1:]), (g_other, other)], left, eigvals, out)


def solution(mesh):
    placed = (
        P(("groups", "dp"), "basis"),
        P(("groups", "dp"), "basis"),
        P("basis", "dp"),
        P("basis", "dp"),
        P("dp", None),
        P(("groups", "dp")),
    )
    chosen = by_swaps if mesh.shape["basis"] == 1 and mesh.shape["dp"] == 16 else general
    return jax.shard_map(
        chosen,
        mesh=mesh,
        in_specs=placed,
        out_specs=P(("groups", "basis"), "dp", None),
        check_vma=False,
    )
```

```python
import functools

import jax
import jax.numpy as jnp
from jax import lax
from jax.experimental import pallas as pl
from jax.experimental.pallas import tpu as pltpu
from jax.sharding import PartitionSpec as P

CAND = 4
KBLK = 1024
RBLK = 256
FLIGHT = 3
PROJECT_VMEM = 14 << 20
OUTER_VMEM = 50 << 20
PARTS = 4


def general(factors_in, factors_out, basis_in, basis_out, eigvals, live_counts):
    slot_rows = factors_in.shape[0]
    keep = (lax.iota(jnp.int32, slot_rows) < live_counts[0])[:, None]
    masked = jnp.where(keep, factors_in, jnp.zeros_like(factors_in))
    partial_in = jnp.dot(
        lax.all_gather(masked, "dp", axis=0, tiled=True),
        basis_in,
        preferred_element_type=jnp.float32,
    )
    partial_out = jnp.dot(
        lax.all_gather(factors_out, "dp", axis=0, tiled=True),
        basis_out,
        preferred_element_type=jnp.float32,
    )
    halves = lax.axis_size("basis")
    share = partial_in.shape[0] // halves
    summed_in, summed_out = lax.psum((partial_in, partial_out), "basis")
    first = lax.axis_index("basis") * share
    proj_in = lax.dynamic_slice_in_dim(summed_in, first, share, 0).astype(jnp.bfloat16)
    proj_out = lax.dynamic_slice_in_dim(summed_out, first, share, 0).astype(jnp.bfloat16)
    cand_local = CAND // halves
    per_cand = share // cand_local
    pout_grouped = proj_out.reshape(cand_local, per_cand, proj_out.shape[1])
    shifted = eigvals.astype(jnp.float32) + 0.01
    piece = lax.all_gather(proj_in, "dp", axis=1, tiled=True)
    pin_grouped = piece.reshape(cand_local, per_cand, piece.shape[1])
    summed = jnp.einsum(
        "ati,atj->aij", pout_grouped, pin_grouped, preferred_element_type=jnp.float32
    )
    return (summed / shifted[None, :, :]).astype(jnp.bfloat16)


def swap(x, m):
    n = lax.axis_size("dp")
    return lax.ppermute(x, "dp", [(d, d ^ m) for d in range(n)])


def after(x, *others):
    return lax.optimization_barrier((x,) + others)[0]


def project_kernel(blocks, which, turn, own_ref, *refs):
    count = len(blocks)
    sources, basis_ref, out_ref = refs[:count], refs[count], refs[count + 1]
    pieces, (held, rows, sems, piece_sems) = refs[count + 2:-4], refs[-4:]
    chunks, width = held.shape[:2]
    slots = pieces[0].shape[-2]
    copies = [
        pltpu.make_async_copy(source.at[:, which], piece, piece_sems.at[k])
        for k, (source, piece) in enumerate(zip(sources, pieces))
    ]
    reads = [
        pltpu.make_async_copy(basis_ref.at[pl.ds(k * width, width)], held.at[k], sems.at[k])
        for k in range(chunks)
    ]
    reads[0].start()
    for copy in copies:
        copy.start()
    for read in reads[1:]:
        read.start()
    for copy, piece, entries in zip(copies, pieces, blocks):
        copy.wait()
        for e, m in enumerate(entries):
            rows[m * slots:(m + 1) * slots, :] = piece[e].astype(jnp.float32)
    acc = None
    for k in range(chunks):
        reads[k].wait()
        part = jnp.dot(
            rows[:, k * width:(k + 1) * width].astype(jnp.bfloat16),
            held[k],
            preferred_element_type=jnp.float32,
        )
        acc = part if acc is None else acc + part
    total = rows.shape[0]
    to = lax.broadcasted_iota(jnp.int32, (total, total), 0)
    come = lax.broadcasted_iota(jnp.int32, (total, total), 1)
    where = jnp.bitwise_xor(come // slots, own_ref[0]) * slots + come % slots
    pick = jnp.where(to == where, 1.0, 0.0).astype(jnp.bfloat16)
    proj = jnp.dot(pick, acc.astype(jnp.bfloat16), preferred_element_type=jnp.float32)
    if turn:
        turned = proj.T
        token = lax.broadcasted_iota(jnp.int32, turned.shape, 1)
        for c in range(CAND):
            own_tokens = token // (total // CAND) == c
            out_ref[c] = jnp.where(own_tokens, turned, 0.0).astype(jnp.bfloat16)
    else:
        out_ref[...] = proj.astype(jnp.bfloat16)


def anywhere(count):
    return [pl.BlockSpec(memory_space=pl.ANY)] * count


def project(own, blocks, basis, which, turn):
    slots = blocks[0][0].shape[-2]
    depth, cols = basis.shape
    total = slots * sum(len(entries) for _, entries in blocks)
    shape = (CAND, cols, total) if turn else (total, cols)
    chunks = depth // KBLK
    return pl.pallas_call(
        functools.partial(project_kernel, [entries for _, entries in blocks], which, turn),
        out_shape=jax.ShapeDtypeStruct(shape, jnp.bfloat16),
        in_specs=[pl.BlockSpec(memory_space=pltpu.SMEM)] + anywhere(len(blocks) + 1),
        out_specs=pl.BlockSpec(memory_space=pltpu.VMEM),
        scratch_shapes=[
            pltpu.VMEM((len(entries), slots, depth), jnp.bfloat16) for _, entries in blocks
        ] + [
            pltpu.VMEM((chunks, KBLK, cols), jnp.bfloat16),
            pltpu.VMEM((total, depth), jnp.float32),
            pltpu.SemaphoreType.DMA((chunks,)),
            pltpu.SemaphoreType.DMA((len(blocks),)),
        ],
        compiler_params=pltpu.CompilerParams(vmem_limit_bytes=PROJECT_VMEM),
        cost_estimate=pl.CostEstimate(flops=total, bytes_accessed=total, transcendentals=0),
    )(own, *[x for x, _ in blocks], basis)


def outer_kernel(blocks, own_ref, *refs):
    given = len(blocks)
    sources, left_any, eig_ref = refs[:given], refs[given], refs[given + 1]
    out_ref, left, right, eig, out, eig_sems, out_sems, piece_sems, left_sem = refs[-9:]
    order = [m for entries in blocks for m in entries]
    count = len(order)
    rows, cols = eig.shape[1:]
    depth = out.shape[0]

    def columns(s):
        m = jnp.int32(order[0])
        for k in range(1, count):
            m = jnp.where(s == k, order[k], m)
        return pl.ds(pl.multiple_of(jnp.bitwise_xor(m, own_ref[0]) * cols, cols), cols)

    def read(s):
        return pltpu.make_async_copy(eig_ref.at[:, columns(s)], eig.at[s], eig_sems.at[s])

    def write(s, c):
        slot = lax.rem(s, depth)
        return pltpu.make_async_copy(
            out.at[slot, c], out_ref.at[c, :, columns(s)], out_sems.at[slot, c]
        )

    copies, at = [pltpu.make_async_copy(left_any, left, left_sem)], 0
    for k, (source, entries) in enumerate(zip(sources, blocks)):
        room = right.at[pl.ds(at, len(entries))]
        copies.append(pltpu.make_async_copy(source, room, piece_sems.at[k]))
        at += len(entries)
    read(0).start()
    for copy in copies:
        copy.start()
    for s in range(1, count):
        read(s).start()
    for copy in copies:
        copy.wait()

    def work(s, slot):
        read(s).wait()
        for r in range(0, rows, RBLK):
            shifted = eig[s, r:r + RBLK, :].astype(jnp.float32) + 0.01
            near = pl.reciprocal(shifted, approx=True)
            scale = near * (2.0 - shifted * near)
            for c in range(CAND):
                summed = jnp.dot(
                    left[c, r:r + RBLK, :], right[s], preferred_element_type=jnp.float32
                )
                out[slot, c, r:r + RBLK, :] = (summed * scale).astype(jnp.bfloat16)
        for c in range(CAND):
            write(s, c).start()

    for s in range(depth):
        work(s, s)

    @pl.loop(depth, count)
    def _(s):
        for c in range(CAND):
            write(s - depth, c).wait()
        work(s, lax.rem(s, depth))

    for s in range(max(0, count - depth), count):
        for c in range(CAND):
            write(s, c).wait()


def outer(own, blocks, left, eigvals, before):
    total, cols = blocks[0][0].shape[-2:]
    rows, width = eigvals.shape
    count = sum(len(entries) for _, entries in blocks)
    operands = [own] + [x for x, _ in blocks] + [left, eigvals]
    aliases = {}
    if before is not None:
        aliases = {len(operands): 0}
        operands.append(before)
    share = count * cols
    return pl.pallas_call(
        functools.partial(outer_kernel, [entries for _, entries in blocks]),
        out_shape=jax.ShapeDtypeStruct((CAND, rows, width), jnp.bfloat16),
        in_specs=[pl.BlockSpec(memory_space=pltpu.SMEM)] + anywhere(len(operands) - 1),
        out_specs=pl.BlockSpec(memory_space=pl.ANY),
        scratch_shapes=[
            pltpu.VMEM(left.shape, jnp.bfloat16),
            pltpu.VMEM((count, total, cols), jnp.bfloat16),
            pltpu.VMEM((count, rows, cols), jnp.bfloat16),
            pltpu.VMEM((FLIGHT, CAND, rows, cols), jnp.bfloat16),
            pltpu.SemaphoreType.DMA((count,)),
            pltpu.SemaphoreType.DMA((FLIGHT, CAND)),
            pltpu.SemaphoreType.DMA((len(blocks),)),
            pltpu.SemaphoreType.DMA(()),
        ],
        input_output_aliases=aliases,
        compiler_params=pltpu.CompilerParams(vmem_limit_bytes=OUTER_VMEM),
        cost_estimate=pl.CostEstimate(
            flops=2 * total * rows * share,
            bytes_accessed=2 * rows * share * (CAND + 1),
            transcendentals=rows * share,
        ),
    )(*operands)


def stage_kernel(count, *refs):
    sources, (ready_ref, *kept), sems = refs[:count], refs[count:-1], refs[-1]
    copies = []
    for k, (source, keep) in enumerate(zip(sources, kept)):
        part = source.shape[0] // PARTS
        for p in range(PARTS):
            rows = pl.ds(p * part, part)
            copies.append(pltpu.make_async_copy(source.at[rows], keep.at[rows], sems.at[k, p]))
    for copy in copies:
        copy.start()
    for copy in copies:
        copy.wait()


def stage(arrays, ready):
    return pl.pallas_call(
        functools.partial(stage_kernel, len(arrays)),
        out_shape=[pltpu.VMEM(x.shape, x.dtype) for x in arrays],
        in_specs=anywhere(len(arrays) + 1),
        out_specs=anywhere(len(arrays)),
        scratch_shapes=[pltpu.SemaphoreType.DMA((len(arrays), PARTS))],
        compiler_params=pltpu.CompilerParams(vmem_limit_bytes=1 << 20),
        cost_estimate=pl.CostEstimate(flops=1, bytes_accessed=1, transcendentals=0),
    )(*[pltpu.with_memory_space_constraint(x, pltpu.HBM) for x in arrays], ready)


def by_swaps(factors_in, factors_out, basis_in, basis_out, eigvals, live_counts):
    own = lax.axis_index("dp").astype(jnp.int32)[None]
    column = (0, 4, 8, 12)
    pair = (2, 6, 10, 14)
    core = (1, 5, 9, 13)
    other = (3, 7, 11, 15)
    tie = lax.optimization_barrier

    shape = (2,) + factors_in.shape
    plane, slot = [lax.broadcasted_iota(jnp.int32, shape, k) for k in (0, 1)]
    keep = (plane == 0) | (slot < live_counts[0])
    f = jnp.where(keep, jnp.stack([factors_in, factors_out]), jnp.zeros((), factors_in.dtype))
    f1, fp, f2, f3 = [swap(f, m) for m in (4, 2, 8, 12)]
    f1, fp = tie((f1, fp))
    fp1 = swap(f1, 2)
    basis_in, basis_out = stage([basis_in, basis_out], f1)
    f2, f3, near = tie((f2, f3, fp1, basis_in, basis_out))[:3]
    near = jnp.stack([fp, near])
    far = swap(jnp.stack([f2, f3]), 2)
    f_column = jnp.stack([f, f1, f2, f3])
    f_core = swap(f_column, 1)
    near_core = swap(near, 1)
    far_core = swap(far, 1)
    blocks = [
        (f_column, column), (near, pair[:2]), (f_core, core), (near_core, other[:2]),
        (far, pair[2:]), (far_core, other[2:]),
    ]
    pin = project(own, blocks, basis_in, 0, False)

    g1, g2, g3 = [swap(pin, m) for m in (4, 8, 12)]
    left = project(own, blocks, basis_out, 1, True)
    g1, g2, g3 = tie((g1, g2, g3, left))[:3]
    g_column = jnp.stack([pin, g1, g2, g3])
    g_pair = swap(g_column, 2)
    g_core = swap(g_column, 1)
    out = outer(own, [(g_column, column)], left, eigvals, None)
    g_other = swap(after(g_pair, out), 1)
    return outer(own, [(g_core, core), (g_pair, pair), (g_other, other)], left, eigvals, out)


def solution(mesh):
    placed = (
        P(("groups", "dp"), "basis"),
        P(("groups", "dp"), "basis"),
        P("basis", "dp"),
        P("basis", "dp"),
        P("dp", None),
        P(("groups", "dp")),
    )
    chosen = by_swaps if mesh.shape["basis"] == 1 and mesh.shape["dp"] == 16 else general
    return jax.shard_map(
        chosen,
        mesh=mesh,
        in_specs=placed,
        out_specs=P(("groups", "basis"), "dp", None),
        check_vma=False,
    )
```

```python
import functools

import jax
import jax.numpy as jnp
from jax import lax
from jax.experimental import pallas as pl
from jax.experimental.pallas import tpu as pltpu
from jax.sharding import PartitionSpec as P

CAND = 4
KBLK = 1024
RBLK = 256
FLIGHT = 3
VMEM = 50 << 20


def general(factors_in, factors_out, basis_in, basis_out, eigvals, live_counts):
    slot_rows = factors_in.shape[0]
    keep = (lax.iota(jnp.int32, slot_rows) < live_counts[0])[:, None]
    masked = jnp.where(keep, factors_in, jnp.zeros_like(factors_in))
    partial_in = jnp.dot(
        lax.all_gather(masked, "dp", axis=0, tiled=True),
        basis_in,
        preferred_element_type=jnp.float32,
    )
    partial_out = jnp.dot(
        lax.all_gather(factors_out, "dp", axis=0, tiled=True),
        basis_out,
        preferred_element_type=jnp.float32,
    )
    halves = lax.axis_size("basis")
    share = partial_in.shape[0] // halves
    summed_in, summed_out = lax.psum((partial_in, partial_out), "basis")
    first = lax.axis_index("basis") * share
    proj_in = lax.dynamic_slice_in_dim(summed_in, first, share, 0).astype(jnp.bfloat16)
    proj_out = lax.dynamic_slice_in_dim(summed_out, first, share, 0).astype(jnp.bfloat16)
    cand_local = CAND // halves
    per_cand = share // cand_local
    pout_grouped = proj_out.reshape(cand_local, per_cand, proj_out.shape[1])
    shifted = eigvals.astype(jnp.float32) + 0.01
    piece = lax.all_gather(proj_in, "dp", axis=1, tiled=True)
    pin_grouped = piece.reshape(cand_local, per_cand, piece.shape[1])
    summed = jnp.einsum(
        "ati,atj->aij", pout_grouped, pin_grouped, preferred_element_type=jnp.float32
    )
    return (summed / shifted[None, :, :]).astype(jnp.bfloat16)


def swap(x, m):
    n = lax.axis_size("dp")
    return lax.ppermute(x, "dp", [(d, d ^ m) for d in range(n)])


def after(x, *others):
    return lax.optimization_barrier((x,) + others)[0]


def project_kernel(blocks, which, turn, own_ref, *refs):
    count = len(blocks)
    sources, basis_ref, out_ref = refs[:count], refs[count], refs[count + 1]
    pieces, (held, rows, sems, piece_sems) = refs[count + 2:-4], refs[-4:]
    chunks, width = held.shape[:2]
    slots = pieces[0].shape[-2]
    copies = [
        pltpu.make_async_copy(source.at[:, which], piece, piece_sems.at[k])
        for k, (source, piece) in enumerate(zip(sources, pieces))
    ]
    reads = [
        pltpu.make_async_copy(basis_ref.at[pl.ds(k * width, width)], held.at[k], sems.at[k])
        for k in range(chunks)
    ]
    reads[0].start()
    for copy in copies:
        copy.start()
    for read in reads[1:]:
        read.start()
    for copy, piece, entries in zip(copies, pieces, blocks):
        copy.wait()
        for e, m in enumerate(entries):
            rows[m * slots:(m + 1) * slots, :] = piece[e].astype(jnp.float32)
    acc = None
    for k in range(chunks):
        reads[k].wait()
        part = jnp.dot(
            rows[:, k * width:(k + 1) * width].astype(jnp.bfloat16),
            held[k],
            preferred_element_type=jnp.float32,
        )
        acc = part if acc is None else acc + part
    total = rows.shape[0]
    to = lax.broadcasted_iota(jnp.int32, (total, total), 0)
    come = lax.broadcasted_iota(jnp.int32, (total, total), 1)
    where = jnp.bitwise_xor(come // slots, own_ref[0]) * slots + come % slots
    pick = jnp.where(to == where, 1.0, 0.0).astype(jnp.bfloat16)
    proj = jnp.dot(pick, acc.astype(jnp.bfloat16), preferred_element_type=jnp.float32)
    if turn:
        turned = proj.T
        token = lax.broadcasted_iota(jnp.int32, turned.shape, 1)
        for c in range(CAND):
            own_tokens = token // (total // CAND) == c
            out_ref[c] = jnp.where(own_tokens, turned, 0.0).astype(jnp.bfloat16)
    else:
        out_ref[...] = proj.astype(jnp.bfloat16)


def anywhere(count):
    return [pl.BlockSpec(memory_space=pl.ANY)] * count


def project(own, blocks, basis, which, turn):
    slots = blocks[0][0].shape[-2]
    depth, cols = basis.shape
    total = slots * sum(len(entries) for _, entries in blocks)
    shape = (CAND, cols, total) if turn else (total, cols)
    chunks = depth // KBLK
    return pl.pallas_call(
        functools.partial(project_kernel, [entries for _, entries in blocks], which, turn),
        out_shape=jax.ShapeDtypeStruct(shape, jnp.bfloat16),
        in_specs=[pl.BlockSpec(memory_space=pltpu.SMEM)] + anywhere(len(blocks) + 1),
        out_specs=pl.BlockSpec(memory_space=pltpu.VMEM),
        scratch_shapes=[
            pltpu.VMEM((len(entries), slots, depth), jnp.bfloat16) for _, entries in blocks
        ] + [
            pltpu.VMEM((chunks, KBLK, cols), jnp.bfloat16),
            pltpu.VMEM((total, depth), jnp.float32),
            pltpu.SemaphoreType.DMA((chunks,)),
            pltpu.SemaphoreType.DMA((len(blocks),)),
        ],
        compiler_params=pltpu.CompilerParams(vmem_limit_bytes=VMEM),
        cost_estimate=pl.CostEstimate(flops=total, bytes_accessed=total, transcendentals=0),
    )(own, *[x for x, _ in blocks], basis)


def outer_kernel(blocks, own_ref, *refs):
    given = len(blocks)
    sources, left_any, eig_ref = refs[:given], refs[given], refs[given + 1]
    out_ref, left, right, eig, out, eig_sems, out_sems, piece_sems, left_sem = refs[-9:]
    order = [m for entries in blocks for m in entries]
    count = len(order)
    rows, cols = eig.shape[1:]
    depth = out.shape[0]

    def columns(s):
        m = jnp.int32(order[0])
        for k in range(1, count):
            m = jnp.where(s == k, order[k], m)
        return pl.ds(pl.multiple_of(jnp.bitwise_xor(m, own_ref[0]) * cols, cols), cols)

    def read(s):
        return pltpu.make_async_copy(eig_ref.at[:, columns(s)], eig.at[s], eig_sems.at[s])

    def write(s, c):
        slot = lax.rem(s, depth)
        return pltpu.make_async_copy(
            out.at[slot, c], out_ref.at[c, :, columns(s)], out_sems.at[slot, c]
        )

    copies, at = [pltpu.make_async_copy(left_any, left, left_sem)], 0
    for k, (source, entries) in enumerate(zip(sources, blocks)):
        room = right.at[pl.ds(at, len(entries))]
        copies.append(pltpu.make_async_copy(source, room, piece_sems.at[k]))
        at += len(entries)
    read(0).start()
    for copy in copies:
        copy.start()
    for s in range(1, count):
        read(s).start()
    for copy in copies:
        copy.wait()

    def work(s, slot):
        read(s).wait()
        for r in range(0, rows, RBLK):
            shifted = eig[s, r:r + RBLK, :].astype(jnp.float32) + 0.01
            near = pl.reciprocal(shifted, approx=True)
            scale = near * (2.0 - shifted * near)
            for c in range(CAND):
                summed = jnp.dot(
                    left[c, r:r + RBLK, :], right[s], preferred_element_type=jnp.float32
                )
                out[slot, c, r:r + RBLK, :] = (summed * scale).astype(jnp.bfloat16)
        for c in range(CAND):
            write(s, c).start()

    for s in range(depth):
        work(s, s)

    @pl.loop(depth, count)
    def _(s):
        for c in range(CAND):
            write(s - depth, c).wait()
        work(s, lax.rem(s, depth))

    for s in range(max(0, count - depth), count):
        for c in range(CAND):
            write(s, c).wait()


def outer(own, blocks, left, eigvals, before):
    total, cols = blocks[0][0].shape[-2:]
    rows, width = eigvals.shape
    count = sum(len(entries) for _, entries in blocks)
    operands = [own] + [x for x, _ in blocks] + [left, eigvals]
    aliases = {}
    if before is not None:
        aliases = {len(operands): 0}
        operands.append(before)
    share = count * cols
    return pl.pallas_call(
        functools.partial(outer_kernel, [entries for _, entries in blocks]),
        out_shape=jax.ShapeDtypeStruct((CAND, rows, width), jnp.bfloat16),
        in_specs=[pl.BlockSpec(memory_space=pltpu.SMEM)] + anywhere(len(operands) - 1),
        out_specs=pl.BlockSpec(memory_space=pl.ANY),
        scratch_shapes=[
            pltpu.VMEM(left.shape, jnp.bfloat16),
            pltpu.VMEM((count, total, cols), jnp.bfloat16),
            pltpu.VMEM((count, rows, cols), jnp.bfloat16),
            pltpu.VMEM((FLIGHT, CAND, rows, cols), jnp.bfloat16),
            pltpu.SemaphoreType.DMA((count,)),
            pltpu.SemaphoreType.DMA((FLIGHT, CAND)),
            pltpu.SemaphoreType.DMA((len(blocks),)),
            pltpu.SemaphoreType.DMA(()),
        ],
        input_output_aliases=aliases,
        compiler_params=pltpu.CompilerParams(vmem_limit_bytes=VMEM),
        cost_estimate=pl.CostEstimate(
            flops=2 * total * rows * share,
            bytes_accessed=2 * rows * share * (CAND + 1),
            transcendentals=rows * share,
        ),
    )(*operands)


def by_swaps(factors_in, factors_out, basis_in, basis_out, eigvals, live_counts):
    own = lax.axis_index("dp").astype(jnp.int32)[None]
    column = (0, 4, 8, 12)
    pair = (2, 6, 10, 14)
    core = (1, 5, 9, 13)
    other = (3, 7, 11, 15)
    tie = lax.optimization_barrier

    shape = (2,) + factors_in.shape
    plane, slot = [lax.broadcasted_iota(jnp.int32, shape, k) for k in (0, 1)]
    keep = (plane == 0) | (slot < live_counts[0])
    f = jnp.where(keep, jnp.stack([factors_in, factors_out]), jnp.zeros((), factors_in.dtype))
    f1, fp, f2, f3 = [swap(f, m) for m in (4, 2, 8, 12)]
    f1, fp = tie((f1, fp))
    fp1 = swap(f1, 2)
    f2, f3, near = tie((f2, f3, fp1))
    near = jnp.stack([fp, near])
    far = swap(jnp.stack([f2, f3]), 2)
    f_column = jnp.stack([f, f1, f2, f3])
    f_core = swap(f_column, 1)
    near_core = swap(near, 1)
    far_core = swap(far, 1)
    blocks = [
        (f_column, column), (near, pair[:2]), (f_core, core), (near_core, other[:2]),
        (far, pair[2:]), (far_core, other[2:]),
    ]
    pin = project(own, blocks, basis_in, 0, False)

    g1, g2, g3 = [swap(pin, m) for m in (4, 8, 12)]
    left = project(own, blocks, basis_out, 1, True)
    g1, g2, g3 = tie((g1, g2, g3, left))[:3]
    g_column = jnp.stack([pin, g1, g2, g3])
    g_pair = swap(g_column, 2)
    g_core = swap(g_column, 1)
    out = outer(own, [(g_column, column)], left, eigvals, None)
    g_other = swap(after(g_pair, out), 1)
    return outer(own, [(g_core, core), (g_pair, pair), (g_other, other)], left, eigvals, out)


def solution(mesh):
    placed = (
        P(("groups", "dp"), "basis"),
        P(("groups", "dp"), "basis"),
        P("basis", "dp"),
        P("basis", "dp"),
        P("dp", None),
        P(("groups", "dp")),
    )
    chosen = by_swaps if mesh.shape["basis"] == 1 and mesh.shape["dp"] == 16 else general
    return jax.shard_map(
        chosen,
        mesh=mesh,
        in_specs=placed,
        out_specs=P(("groups", "basis"), "dp", None),
        check_vma=False,
    )
```

```python
import functools

import jax
import jax.numpy as jnp
from jax import lax
from jax.experimental import pallas as pl
from jax.experimental.pallas import tpu as pltpu
from jax.sharding import PartitionSpec as P

CAND = 4
KBLK = 1024
RBLK = 256
FLIGHT = 3
VMEM = 50 << 20


def general(factors_in, factors_out, basis_in, basis_out, eigvals, live_counts):
    slot_rows = factors_in.shape[0]
    keep = (lax.iota(jnp.int32, slot_rows) < live_counts[0])[:, None]
    masked = jnp.where(keep, factors_in, jnp.zeros_like(factors_in))
    partial_in = jnp.dot(
        lax.all_gather(masked, "dp", axis=0, tiled=True),
        basis_in,
        preferred_element_type=jnp.float32,
    )
    partial_out = jnp.dot(
        lax.all_gather(factors_out, "dp", axis=0, tiled=True),
        basis_out,
        preferred_element_type=jnp.float32,
    )
    halves = lax.axis_size("basis")
    share = partial_in.shape[0] // halves
    summed_in, summed_out = lax.psum((partial_in, partial_out), "basis")
    first = lax.axis_index("basis") * share
    proj_in = lax.dynamic_slice_in_dim(summed_in, first, share, 0).astype(jnp.bfloat16)
    proj_out = lax.dynamic_slice_in_dim(summed_out, first, share, 0).astype(jnp.bfloat16)
    cand_local = CAND // halves
    per_cand = share // cand_local
    pout_grouped = proj_out.reshape(cand_local, per_cand, proj_out.shape[1])
    shifted = eigvals.astype(jnp.float32) + 0.01
    piece = lax.all_gather(proj_in, "dp", axis=1, tiled=True)
    pin_grouped = piece.reshape(cand_local, per_cand, piece.shape[1])
    summed = jnp.einsum(
        "ati,atj->aij", pout_grouped, pin_grouped, preferred_element_type=jnp.float32
    )
    return (summed / shifted[None, :, :]).astype(jnp.bfloat16)


def swap(x, m):
    n = lax.axis_size("dp")
    return lax.ppermute(x, "dp", [(d, d ^ m) for d in range(n)])


def after(x, *others):
    return lax.optimization_barrier((x,) + others)[0]


def project_kernel(blocks, which, turn, own_ref, *refs):
    count = len(blocks)
    sources, basis_ref, out_ref = refs[:count], refs[count], refs[count + 1]
    pieces, (held, rows, sems, piece_sems) = refs[count + 2:-4], refs[-4:]
    chunks, width = held.shape[:2]
    slots = pieces[0].shape[-2]
    copies = [
        pltpu.make_async_copy(
            source if len(source.shape) == 3 else source.at[:, which], piece, piece_sems.at[k]
        )
        for k, (source, piece) in enumerate(zip(sources, pieces))
    ]
    reads = [
        pltpu.make_async_copy(basis_ref.at[pl.ds(k * width, width)], held.at[k], sems.at[k])
        for k in range(chunks)
    ]
    reads[0].start()
    for copy in copies:
        copy.start()
    for read in reads[1:]:
        read.start()
    for copy, piece, entries in zip(copies, pieces, blocks):
        copy.wait()
        for e, m in enumerate(entries):
            rows[m * slots:(m + 1) * slots, :] = piece[e].astype(jnp.float32)
    acc = None
    for k in range(chunks):
        reads[k].wait()
        part = jnp.dot(
            rows[:, k * width:(k + 1) * width].astype(jnp.bfloat16),
            held[k],
            preferred_element_type=jnp.float32,
        )
        acc = part if acc is None else acc + part
    total = rows.shape[0]
    to = lax.broadcasted_iota(jnp.int32, (total, total), 0)
    come = lax.broadcasted_iota(jnp.int32, (total, total), 1)
    where = jnp.bitwise_xor(come // slots, own_ref[0]) * slots + come % slots
    pick = jnp.where(to == where, 1.0, 0.0).astype(jnp.bfloat16)
    proj = jnp.dot(pick, acc.astype(jnp.bfloat16), preferred_element_type=jnp.float32)
    if turn:
        turned = proj.T
        token = lax.broadcasted_iota(jnp.int32, turned.shape, 1)
        for c in range(CAND):
            own_tokens = token // (total // CAND) == c
            out_ref[c] = jnp.where(own_tokens, turned, 0.0).astype(jnp.bfloat16)
    else:
        out_ref[...] = proj.astype(jnp.bfloat16)


def anywhere(count):
    return [pl.BlockSpec(memory_space=pl.ANY)] * count


def project(own, blocks, basis, which, turn):
    slots = blocks[0][0].shape[-2]
    depth, cols = basis.shape
    total = slots * sum(len(entries) for _, entries in blocks)
    shape = (CAND, cols, total) if turn else (total, cols)
    chunks = depth // KBLK
    return pl.pallas_call(
        functools.partial(project_kernel, [entries for _, entries in blocks], which, turn),
        out_shape=jax.ShapeDtypeStruct(shape, jnp.bfloat16),
        in_specs=[pl.BlockSpec(memory_space=pltpu.SMEM)] + anywhere(len(blocks) + 1),
        out_specs=pl.BlockSpec(memory_space=pltpu.VMEM),
        scratch_shapes=[
            pltpu.VMEM((len(entries), slots, depth), jnp.bfloat16) for _, entries in blocks
        ] + [
            pltpu.VMEM((chunks, KBLK, cols), jnp.bfloat16),
            pltpu.VMEM((total, depth), jnp.float32),
            pltpu.SemaphoreType.DMA((chunks,)),
            pltpu.SemaphoreType.DMA((len(blocks),)),
        ],
        compiler_params=pltpu.CompilerParams(vmem_limit_bytes=VMEM),
        cost_estimate=pl.CostEstimate(flops=total, bytes_accessed=total, transcendentals=0),
    )(own, *[x for x, _ in blocks], basis)


def outer_kernel(blocks, own_ref, *refs):
    given = len(blocks)
    sources, left_any, eig_ref = refs[:given], refs[given], refs[given + 1]
    out_ref, left, right, eig, out, eig_sems, out_sems, piece_sems, left_sem = refs[-9:]
    order = [m for entries in blocks for m in entries]
    count = len(order)
    rows, cols = eig.shape[1:]
    depth = out.shape[0]

    def columns(s):
        m = jnp.int32(order[0])
        for k in range(1, count):
            m = jnp.where(s == k, order[k], m)
        return pl.ds(pl.multiple_of(jnp.bitwise_xor(m, own_ref[0]) * cols, cols), cols)

    def read(s):
        return pltpu.make_async_copy(eig_ref.at[:, columns(s)], eig.at[s], eig_sems.at[s])

    def write(s, c):
        slot = lax.rem(s, depth)
        return pltpu.make_async_copy(
            out.at[slot, c], out_ref.at[c, :, columns(s)], out_sems.at[slot, c]
        )

    copies, at = [pltpu.make_async_copy(left_any, left, left_sem)], 0
    for k, (source, entries) in enumerate(zip(sources, blocks)):
        room = right.at[pl.ds(at, len(entries))]
        copies.append(pltpu.make_async_copy(source, room, piece_sems.at[k]))
        at += len(entries)
    read(0).start()
    for copy in copies:
        copy.start()
    for s in range(1, count):
        read(s).start()
    for copy in copies:
        copy.wait()

    def work(s, slot):
        read(s).wait()
        for r in range(0, rows, RBLK):
            shifted = eig[s, r:r + RBLK, :].astype(jnp.float32) + 0.01
            near = pl.reciprocal(shifted, approx=True)
            scale = near * (2.0 - shifted * near)
            for c in range(CAND):
                summed = jnp.dot(
                    left[c, r:r + RBLK, :], right[s], preferred_element_type=jnp.float32
                )
                out[slot, c, r:r + RBLK, :] = (summed * scale).astype(jnp.bfloat16)
        for c in range(CAND):
            write(s, c).start()

    for s in range(depth):
        work(s, s)

    @pl.loop(depth, count)
    def _(s):
        for c in range(CAND):
            write(s - depth, c).wait()
        work(s, lax.rem(s, depth))

    for s in range(max(0, count - depth), count):
        for c in range(CAND):
            write(s, c).wait()


def outer(own, blocks, left, eigvals, before):
    total, cols = blocks[0][0].shape[-2:]
    rows, width = eigvals.shape
    count = sum(len(entries) for _, entries in blocks)
    operands = [own] + [x for x, _ in blocks] + [left, eigvals]
    aliases = {}
    if before is not None:
        aliases = {len(operands): 0}
        operands.append(before)
    share = count * cols
    return pl.pallas_call(
        functools.partial(outer_kernel, [entries for _, entries in blocks]),
        out_shape=jax.ShapeDtypeStruct((CAND, rows, width), jnp.bfloat16),
        in_specs=[pl.BlockSpec(memory_space=pltpu.SMEM)] + anywhere(len(operands) - 1),
        out_specs=pl.BlockSpec(memory_space=pl.ANY),
        scratch_shapes=[
            pltpu.VMEM(left.shape, jnp.bfloat16),
            pltpu.VMEM((count, total, cols), jnp.bfloat16),
            pltpu.VMEM((count, rows, cols), jnp.bfloat16),
            pltpu.VMEM((FLIGHT, CAND, rows, cols), jnp.bfloat16),
            pltpu.SemaphoreType.DMA((count,)),
            pltpu.SemaphoreType.DMA((FLIGHT, CAND)),
            pltpu.SemaphoreType.DMA((len(blocks),)),
            pltpu.SemaphoreType.DMA(()),
        ],
        input_output_aliases=aliases,
        compiler_params=pltpu.CompilerParams(vmem_limit_bytes=VMEM),
        cost_estimate=pl.CostEstimate(
            flops=2 * total * rows * share,
            bytes_accessed=2 * rows * share * (CAND + 1),
            transcendentals=rows * share,
        ),
    )(*operands)


def by_swaps(factors_in, factors_out, basis_in, basis_out, eigvals, live_counts):
    own = lax.axis_index("dp").astype(jnp.int32)[None]
    column = (0, 4, 8, 12)
    pair = (2, 6, 10, 14)
    core = (1, 5, 9, 13)
    other = (3, 7, 11, 15)
    tie = lax.optimization_barrier

    a2, a3 = [swap(factors_in, m) for m in (8, 12)]
    keep = (lax.iota(jnp.int32, factors_in.shape[0]) < live_counts[0])[:, None]
    masked = tie(jnp.where(keep, factors_out, jnp.zeros_like(factors_out)))
    b2, b3 = [swap(masked, m) for m in (8, 12)]
    f = tie(jnp.stack([factors_in, masked]))
    f1, fp = tie((swap(f, 4), swap(f, 2)))
    fp1 = swap(f1, 2)
    a2, a3 = tie((a2, a3))[:2]
    a_far = jnp.stack([a2, a3])
    a_far_pair = swap(a_far, 2)
    a_far_core = swap(a_far, 1)
    near = jnp.stack([f, f1, fp, fp1])
    near_core = swap(near, 1)
    a_far_other = swap(a_far_pair, 1)
    a_far_other, b2, b3 = tie((a_far_other, b2, b3))
    b_far = jnp.stack([b2, b3])
    b_far_pair = swap(b_far, 2)
    joined = [(near, (0, 4, 2, 6)), (near_core, (1, 5, 3, 7))]
    pin = project(
        own,
        joined + [
            (a_far, column[2:]), (a_far_pair, pair[2:]), (a_far_core, core[2:]),
            (a_far_other, other[2:]),
        ],
        basis_in, 0, False,
    )

    b_far_pair = after(b_far_pair, pin)
    b_far = jnp.concatenate([b_far, b_far_pair])
    b_far_core = swap(b_far, 1)
    blocks = joined + [(b_far, column[2:] + pair[2:]), (b_far_core, core[2:] + other[2:])]
    g1, g2, g3 = [swap(pin, m) for m in (4, 8, 12)]
    left = project(own, blocks, basis_out, 1, True)
    g1, g2, g3 = tie((g1, g2, g3, left))[:3]
    g_column = jnp.stack([pin, g1, g2, g3])
    g_pair = swap(g_column, 2)
    g_core = swap(g_column, 1)
    out = outer(own, [(g_column, column)], left, eigvals, None)
    g_other = swap(after(g_pair, out), 1)
    return outer(own, [(g_core, core), (g_pair, pair), (g_other, other)], left, eigvals, out)


def solution(mesh):
    placed = (
        P(("groups", "dp"), "basis"),
        P(("groups", "dp"), "basis"),
        P("basis", "dp"),
        P("basis", "dp"),
        P("dp", None),
        P(("groups", "dp")),
    )
    chosen = by_swaps if mesh.shape["basis"] == 1 and mesh.shape["dp"] == 16 else general
    return jax.shard_map(
        chosen,
        mesh=mesh,
        in_specs=placed,
        out_specs=P(("groups", "basis"), "dp", None),
        check_vma=False,
    )
```

```python
import functools

import jax
import jax.numpy as jnp
from jax import lax
from jax.experimental import pallas as pl
from jax.experimental.pallas import tpu as pltpu
from jax.sharding import PartitionSpec as P

CAND = 4
KBLK = 1024
RBLK = 256
FLIGHT = 4
VMEM = 50 << 20


def general(factors_in, factors_out, basis_in, basis_out, eigvals, live_counts):
    slot_rows = factors_in.shape[0]
    keep = (lax.iota(jnp.int32, slot_rows) < live_counts[0])[:, None]
    masked = jnp.where(keep, factors_in, jnp.zeros_like(factors_in))
    partial_in = jnp.dot(
        lax.all_gather(masked, "dp", axis=0, tiled=True),
        basis_in,
        preferred_element_type=jnp.float32,
    )
    partial_out = jnp.dot(
        lax.all_gather(factors_out, "dp", axis=0, tiled=True),
        basis_out,
        preferred_element_type=jnp.float32,
    )
    halves = lax.axis_size("basis")
    share = partial_in.shape[0] // halves
    summed_in, summed_out = lax.psum((partial_in, partial_out), "basis")
    first = lax.axis_index("basis") * share
    proj_in = lax.dynamic_slice_in_dim(summed_in, first, share, 0).astype(jnp.bfloat16)
    proj_out = lax.dynamic_slice_in_dim(summed_out, first, share, 0).astype(jnp.bfloat16)
    cand_local = CAND // halves
    per_cand = share // cand_local
    pout_grouped = proj_out.reshape(cand_local, per_cand, proj_out.shape[1])
    shifted = eigvals.astype(jnp.float32) + 0.01
    piece = lax.all_gather(proj_in, "dp", axis=1, tiled=True)
    pin_grouped = piece.reshape(cand_local, per_cand, piece.shape[1])
    summed = jnp.einsum(
        "ati,atj->aij", pout_grouped, pin_grouped, preferred_element_type=jnp.float32
    )
    return (summed / shifted[None, :, :]).astype(jnp.bfloat16)


def swap(x, m):
    n = lax.axis_size("dp")
    return lax.ppermute(x, "dp", [(d, d ^ m) for d in range(n)])


def after(x, *others):
    return lax.optimization_barrier((x,) + others)[0]


def project_kernel(blocks, which, turn, own_ref, *refs):
    count = len(blocks)
    sources, basis_ref, out_ref = refs[:count], refs[count], refs[count + 1]
    pieces, (held, rows, sems, piece_sems) = refs[count + 2:-4], refs[-4:]
    chunks, width = held.shape[:2]
    slots = pieces[0].shape[-2]
    copies = [
        pltpu.make_async_copy(
            source if len(source.shape) == 3 else source.at[:, which], piece, piece_sems.at[k]
        )
        for k, (source, piece) in enumerate(zip(sources, pieces))
    ]
    reads = [
        pltpu.make_async_copy(basis_ref.at[pl.ds(k * width, width)], held.at[k], sems.at[k])
        for k in range(chunks)
    ]
    reads[0].start()
    for copy in copies:
        copy.start()
    for read in reads[1:]:
        read.start()
    for copy, piece, entries in zip(copies, pieces, blocks):
        copy.wait()
        for e, m in enumerate(entries):
            rows[m * slots:(m + 1) * slots, :] = piece[e].astype(jnp.float32)
    acc = None
    for k in range(chunks):
        reads[k].wait()
        part = jnp.dot(
            rows[:, k * width:(k + 1) * width].astype(jnp.bfloat16),
            held[k],
            preferred_element_type=jnp.float32,
        )
        acc = part if acc is None else acc + part
    total = rows.shape[0]
    to = lax.broadcasted_iota(jnp.int32, (total, total), 0)
    come = lax.broadcasted_iota(jnp.int32, (total, total), 1)
    where = jnp.bitwise_xor(come // slots, own_ref[0]) * slots + come % slots
    pick = jnp.where(to == where, 1.0, 0.0).astype(jnp.bfloat16)
    proj = jnp.dot(pick, acc.astype(jnp.bfloat16), preferred_element_type=jnp.float32)
    if turn:
        turned = proj.T
        token = lax.broadcasted_iota(jnp.int32, turned.shape, 1)
        for c in range(CAND):
            own_tokens = token // (total // CAND) == c
            out_ref[c] = jnp.where(own_tokens, turned, 0.0).astype(jnp.bfloat16)
    else:
        out_ref[...] = proj.astype(jnp.bfloat16)


def anywhere(count):
    return [pl.BlockSpec(memory_space=pl.ANY)] * count


def project(own, blocks, basis, which, turn):
    slots = blocks[0][0].shape[-2]
    depth, cols = basis.shape
    total = slots * sum(len(entries) for _, entries in blocks)
    shape = (CAND, cols, total) if turn else (total, cols)
    chunks = depth // KBLK
    return pl.pallas_call(
        functools.partial(project_kernel, [entries for _, entries in blocks], which, turn),
        out_shape=jax.ShapeDtypeStruct(shape, jnp.bfloat16),
        in_specs=[pl.BlockSpec(memory_space=pltpu.SMEM)] + anywhere(len(blocks) + 1),
        out_specs=pl.BlockSpec(memory_space=pltpu.VMEM),
        scratch_shapes=[
            pltpu.VMEM((len(entries), slots, depth), jnp.bfloat16) for _, entries in blocks
        ] + [
            pltpu.VMEM((chunks, KBLK, cols), jnp.bfloat16),
            pltpu.VMEM((total, depth), jnp.float32),
            pltpu.SemaphoreType.DMA((chunks,)),
            pltpu.SemaphoreType.DMA((len(blocks),)),
        ],
        compiler_params=pltpu.CompilerParams(vmem_limit_bytes=VMEM),
        cost_estimate=pl.CostEstimate(flops=total, bytes_accessed=total, transcendentals=0),
    )(own, *[x for x, _ in blocks], basis)


def outer_kernel(blocks, own_ref, *refs):
    given = len(blocks)
    sources, left_any, eig_ref = refs[:given], refs[given], refs[given + 1]
    out_ref, left, right, eig, out, eig_sems, out_sems, piece_sems, left_sem = refs[-9:]
    order = [m for entries in blocks for m in entries]
    count = len(order)
    rows, cols = eig.shape[1:]
    depth = out.shape[0]

    def columns(s):
        m = jnp.int32(order[0])
        for k in range(1, count):
            m = jnp.where(s == k, order[k], m)
        return pl.ds(pl.multiple_of(jnp.bitwise_xor(m, own_ref[0]) * cols, cols), cols)

    def read(s):
        return pltpu.make_async_copy(eig_ref.at[:, columns(s)], eig.at[s], eig_sems.at[s])

    def write(s, c):
        slot = lax.rem(s, depth)
        return pltpu.make_async_copy(
            out.at[slot, c], out_ref.at[c, :, columns(s)], out_sems.at[slot, c]
        )

    copies, at = [pltpu.make_async_copy(left_any, left, left_sem)], 0
    for k, (source, entries) in enumerate(zip(sources, blocks)):
        room = right.at[pl.ds(at, len(entries))]
        copies.append(pltpu.make_async_copy(source, room, piece_sems.at[k]))
        at += len(entries)
    read(0).start()
    for copy in copies:
        copy.start()
    for s in range(1, count):
        read(s).start()
    for copy in copies:
        copy.wait()

    def work(s, slot):
        read(s).wait()
        for r in range(0, rows, RBLK):
            shifted = eig[s, r:r + RBLK, :].astype(jnp.float32) + 0.01
            near = pl.reciprocal(shifted, approx=True)
            scale = near * (2.0 - shifted * near)
            for c in range(CAND):
                summed = jnp.dot(
                    left[c, r:r + RBLK, :], right[s], preferred_element_type=jnp.float32
                )
                out[slot, c, r:r + RBLK, :] = (summed * scale).astype(jnp.bfloat16)
        for c in range(CAND):
            write(s, c).start()

    for s in range(depth):
        work(s, s)

    @pl.loop(depth, count)
    def _(s):
        for c in range(CAND):
            write(s - depth, c).wait()
        work(s, lax.rem(s, depth))

    for s in range(max(0, count - depth), count):
        for c in range(CAND):
            write(s, c).wait()


def outer(own, blocks, left, eigvals, before):
    total, cols = blocks[0][0].shape[-2:]
    rows, width = eigvals.shape
    count = sum(len(entries) for _, entries in blocks)
    operands = [own] + [x for x, _ in blocks] + [left, eigvals]
    aliases = {}
    if before is not None:
        aliases = {len(operands): 0}
        operands.append(before)
    share = count * cols
    return pl.pallas_call(
        functools.partial(outer_kernel, [entries for _, entries in blocks]),
        out_shape=jax.ShapeDtypeStruct((CAND, rows, width), jnp.bfloat16),
        in_specs=[pl.BlockSpec(memory_space=pltpu.SMEM)] + anywhere(len(operands) - 1),
        out_specs=pl.BlockSpec(memory_space=pl.ANY),
        scratch_shapes=[
            pltpu.VMEM(left.shape, jnp.bfloat16),
            pltpu.VMEM((count, total, cols), jnp.bfloat16),
            pltpu.VMEM((count, rows, cols), jnp.bfloat16),
            pltpu.VMEM((FLIGHT, CAND, rows, cols), jnp.bfloat16),
            pltpu.SemaphoreType.DMA((count,)),
            pltpu.SemaphoreType.DMA((FLIGHT, CAND)),
            pltpu.SemaphoreType.DMA((len(blocks),)),
            pltpu.SemaphoreType.DMA(()),
        ],
        input_output_aliases=aliases,
        compiler_params=pltpu.CompilerParams(vmem_limit_bytes=VMEM),
        cost_estimate=pl.CostEstimate(
            flops=2 * total * rows * share,
            bytes_accessed=2 * rows * share * (CAND + 1),
            transcendentals=rows * share,
        ),
    )(*operands)


def by_swaps(factors_in, factors_out, basis_in, basis_out, eigvals, live_counts):
    own = lax.axis_index("dp").astype(jnp.int32)[None]
    column = (0, 4, 8, 12)
    pair = (2, 6, 10, 14)
    core = (1, 5, 9, 13)
    other = (3, 7, 11, 15)
    tie = lax.optimization_barrier

    a2, a3 = [swap(factors_in, m) for m in (8, 12)]
    shape = (2,) + factors_in.shape
    plane, slot = [lax.broadcasted_iota(jnp.int32, shape, k) for k in (0, 1)]
    keep = (plane == 0) | (slot < live_counts[0])
    zero = jnp.zeros((), factors_in.dtype)
    f = tie(jnp.where(keep, jnp.stack([factors_in, factors_out]), zero))
    b2, b3 = [swap(f[1], m) for m in (8, 12)]
    f1, fp = tie((swap(f, 4), swap(f, 2)))
    fp1 = swap(f1, 2)
    a2, a3 = tie((a2, a3))[:2]
    a_far = jnp.stack([a2, a3])
    a_far_pair = swap(a_far, 2)
    a_far_core = swap(a_far, 1)
    near = jnp.stack([f, f1, fp, fp1])
    near_core = swap(near, 1)
    a_far_other = swap(a_far_pair, 1)
    a_far_other, b2, b3 = tie((a_far_other, b2, b3))
    b_far = jnp.stack([b2, b3])
    b_far_pair = swap(b_far, 2)
    joined = [(near, (0, 4, 2, 6)), (near_core, (1, 5, 3, 7))]
    pin = project(
        own,
        joined + [
            (a_far, column[2:]), (a_far_pair, pair[2:]), (a_far_core, core[2:]),
            (a_far_other, other[2:]),
        ],
        basis_in, 0, False,
    )

    b_far_pair = after(b_far_pair, pin)
    b_far = jnp.concatenate([b_far, b_far_pair])
    b_far_core = swap(b_far, 1)
    blocks = joined + [(b_far, column[2:] + pair[2:]), (b_far_core, core[2:] + other[2:])]
    g1, g2, g3 = [swap(pin, m) for m in (4, 8, 12)]
    left = project(own, blocks, basis_out, 1, True)
    g1, g2, g3 = tie((g1, g2, g3, left))[:3]
    g_column = jnp.stack([pin, g1, g2, g3])
    g_pair = swap(g_column, 2)
    out = outer(own, [(g_column, column)], left, eigvals, None)
    g_core = swap(after(g_column, out), 1)
    g_other = swap(after(g_pair, out), 1)
    return outer(own, [(g_core, core), (g_pair, pair), (g_other, other)], left, eigvals, out)


def solution(mesh):
    placed = (
        P(("groups", "dp"), "basis"),
        P(("groups", "dp"), "basis"),
        P("basis", "dp"),
        P("basis", "dp"),
        P("dp", None),
        P(("groups", "dp")),
    )
    chosen = by_swaps if mesh.shape["basis"] == 1 and mesh.shape["dp"] == 16 else general
    return jax.shard_map(
        chosen,
        mesh=mesh,
        in_specs=placed,
        out_specs=P(("groups", "basis"), "dp", None),
        check_vma=False,
    )
```

```python
import functools

import jax
import jax.numpy as jnp
from jax import lax
from jax.experimental import pallas as pl
from jax.experimental.pallas import tpu as pltpu
from jax.sharding import PartitionSpec as P

CAND = 4
KBLK = 1024
RBLK = 256
FLIGHT = 4
VMEM = 50 << 20


def general(factors_in, factors_out, basis_in, basis_out, eigvals, live_counts):
    slot_rows = factors_in.shape[0]
    keep = (lax.iota(jnp.int32, slot_rows) < live_counts[0])[:, None]
    masked = jnp.where(keep, factors_in, jnp.zeros_like(factors_in))
    partial_in = jnp.dot(
        lax.all_gather(masked, "dp", axis=0, tiled=True),
        basis_in,
        preferred_element_type=jnp.float32,
    )
    partial_out = jnp.dot(
        lax.all_gather(factors_out, "dp", axis=0, tiled=True),
        basis_out,
        preferred_element_type=jnp.float32,
    )
    halves = lax.axis_size("basis")
    share = partial_in.shape[0] // halves
    summed_in, summed_out = lax.psum((partial_in, partial_out), "basis")
    first = lax.axis_index("basis") * share
    proj_in = lax.dynamic_slice_in_dim(summed_in, first, share, 0).astype(jnp.bfloat16)
    proj_out = lax.dynamic_slice_in_dim(summed_out, first, share, 0).astype(jnp.bfloat16)
    cand_local = CAND // halves
    per_cand = share // cand_local
    pout_grouped = proj_out.reshape(cand_local, per_cand, proj_out.shape[1])
    shifted = eigvals.astype(jnp.float32) + 0.01
    piece = lax.all_gather(proj_in, "dp", axis=1, tiled=True)
    pin_grouped = piece.reshape(cand_local, per_cand, piece.shape[1])
    summed = jnp.einsum(
        "ati,atj->aij", pout_grouped, pin_grouped, preferred_element_type=jnp.float32
    )
    return (summed / shifted[None, :, :]).astype(jnp.bfloat16)


def swap(x, m):
    n = lax.axis_size("dp")
    return lax.ppermute(x, "dp", [(d, d ^ m) for d in range(n)])


def after(x, *others):
    return lax.optimization_barrier((x,) + others)[0]


def project_kernel(blocks, which, turn, own_ref, *refs):
    count = len(blocks)
    sources, basis_ref, out_ref = refs[:count], refs[count], refs[count + 1]
    pieces, (held, rows, sems, piece_sems) = refs[count + 2:-4], refs[-4:]
    chunks, width = held.shape[:2]
    slots = pieces[0].shape[-2]
    copies = [
        pltpu.make_async_copy(
            source if len(source.shape) == 3 else source.at[:, which], piece, piece_sems.at[k]
        )
        for k, (source, piece) in enumerate(zip(sources, pieces))
    ]
    reads = [
        pltpu.make_async_copy(basis_ref.at[pl.ds(k * width, width)], held.at[k], sems.at[k])
        for k in range(chunks)
    ]
    reads[0].start()
    for copy in copies:
        copy.start()
    for read in reads[1:]:
        read.start()
    for copy, piece, entries in zip(copies, pieces, blocks):
        copy.wait()
        for e, m in enumerate(entries):
            rows[m * slots:(m + 1) * slots, :] = piece[e].astype(jnp.float32)
    acc = None
    for k in range(chunks):
        reads[k].wait()
        part = jnp.dot(
            rows[:, k * width:(k + 1) * width].astype(jnp.bfloat16),
            held[k],
            preferred_element_type=jnp.float32,
        )
        acc = part if acc is None else acc + part
    total = rows.shape[0]
    to = lax.broadcasted_iota(jnp.int32, (total, total), 0)
    come = lax.broadcasted_iota(jnp.int32, (total, total), 1)
    where = jnp.bitwise_xor(come // slots, own_ref[0]) * slots + come % slots
    pick = jnp.where(to == where, 1.0, 0.0).astype(jnp.bfloat16)
    proj = jnp.dot(pick, acc.astype(jnp.bfloat16), preferred_element_type=jnp.float32)
    if turn:
        turned = proj.T
        token = lax.broadcasted_iota(jnp.int32, turned.shape, 1)
        for c in range(CAND):
            own_tokens = token // (total // CAND) == c
            out_ref[c] = jnp.where(own_tokens, turned, 0.0).astype(jnp.bfloat16)
    else:
        out_ref[...] = proj.astype(jnp.bfloat16)


def anywhere(count):
    return [pl.BlockSpec(memory_space=pl.ANY)] * count


def project(own, blocks, basis, which, turn):
    slots = blocks[0][0].shape[-2]
    depth, cols = basis.shape
    total = slots * sum(len(entries) for _, entries in blocks)
    shape = (CAND, cols, total) if turn else (total, cols)
    chunks = depth // KBLK
    return pl.pallas_call(
        functools.partial(project_kernel, [entries for _, entries in blocks], which, turn),
        out_shape=jax.ShapeDtypeStruct(shape, jnp.bfloat16),
        in_specs=[pl.BlockSpec(memory_space=pltpu.SMEM)] + anywhere(len(blocks) + 1),
        out_specs=pl.BlockSpec(memory_space=pltpu.VMEM),
        scratch_shapes=[
            pltpu.VMEM((len(entries), slots, depth), jnp.bfloat16) for _, entries in blocks
        ] + [
            pltpu.VMEM((chunks, KBLK, cols), jnp.bfloat16),
            pltpu.VMEM((total, depth), jnp.float32),
            pltpu.SemaphoreType.DMA((chunks,)),
            pltpu.SemaphoreType.DMA((len(blocks),)),
        ],
        compiler_params=pltpu.CompilerParams(vmem_limit_bytes=VMEM),
        cost_estimate=pl.CostEstimate(flops=total, bytes_accessed=total, transcendentals=0),
    )(own, *[x for x, _ in blocks], basis)


def outer_kernel(blocks, own_ref, *refs):
    given = len(blocks)
    sources, left_any, eig_ref = refs[:given], refs[given], refs[given + 1]
    out_ref, left, right, eig, out, eig_sems, out_sems, piece_sems, left_sem = refs[-9:]
    order = [m for entries in blocks for m in entries]
    count = len(order)
    rows, cols = eig.shape[1:]
    depth = out.shape[0]

    def columns(s):
        m = jnp.int32(order[0])
        for k in range(1, count):
            m = jnp.where(s == k, order[k], m)
        return pl.ds(pl.multiple_of(jnp.bitwise_xor(m, own_ref[0]) * cols, cols), cols)

    def read(s):
        return pltpu.make_async_copy(eig_ref.at[:, columns(s)], eig.at[s], eig_sems.at[s])

    def write(s, r, c):
        slot, part = lax.rem(s, depth), pl.ds(r, RBLK)
        return pltpu.make_async_copy(
            out.at[slot, c, part],
            out_ref.at[c, part, columns(s)],
            out_sems.at[slot, r // RBLK, c],
        )

    parts = [(r, c) for r in range(0, rows, RBLK) for c in range(CAND)]

    copies, at = [pltpu.make_async_copy(left_any, left, left_sem)], 0
    for k, (source, entries) in enumerate(zip(sources, blocks)):
        room = right.at[pl.ds(at, len(entries))]
        copies.append(pltpu.make_async_copy(source, room, piece_sems.at[k]))
        at += len(entries)
    read(0).start()
    for copy in copies:
        copy.start()
    for s in range(1, count):
        read(s).start()
    for copy in copies:
        copy.wait()

    def work(s, slot):
        read(s).wait()
        for r in range(0, rows, RBLK):
            shifted = eig[s, r:r + RBLK, :].astype(jnp.float32) + 0.01
            near = pl.reciprocal(shifted, approx=True)
            scale = near * (2.0 - shifted * near)
            for c in range(CAND):
                summed = jnp.dot(
                    left[c, r:r + RBLK, :], right[s], preferred_element_type=jnp.float32
                )
                out[slot, c, r:r + RBLK, :] = (summed * scale).astype(jnp.bfloat16)
            for c in range(CAND):
                write(s, r, c).start()

    for s in range(depth):
        work(s, s)

    @pl.loop(depth, count)
    def _(s):
        for r, c in parts:
            write(s - depth, r, c).wait()
        work(s, lax.rem(s, depth))

    for s in range(max(0, count - depth), count):
        for r, c in parts:
            write(s, r, c).wait()


def outer(own, blocks, left, eigvals, before):
    total, cols = blocks[0][0].shape[-2:]
    rows, width = eigvals.shape
    count = sum(len(entries) for _, entries in blocks)
    operands = [own] + [x for x, _ in blocks] + [left, eigvals]
    aliases = {}
    if before is not None:
        aliases = {len(operands): 0}
        operands.append(before)
    share = count * cols
    return pl.pallas_call(
        functools.partial(outer_kernel, [entries for _, entries in blocks]),
        out_shape=jax.ShapeDtypeStruct((CAND, rows, width), jnp.bfloat16),
        in_specs=[pl.BlockSpec(memory_space=pltpu.SMEM)] + anywhere(len(operands) - 1),
        out_specs=pl.BlockSpec(memory_space=pl.ANY),
        scratch_shapes=[
            pltpu.VMEM(left.shape, jnp.bfloat16),
            pltpu.VMEM((count, total, cols), jnp.bfloat16),
            pltpu.VMEM((count, rows, cols), jnp.bfloat16),
            pltpu.VMEM((FLIGHT, CAND, rows, cols), jnp.bfloat16),
            pltpu.SemaphoreType.DMA((count,)),
            pltpu.SemaphoreType.DMA((FLIGHT, rows // RBLK, CAND)),
            pltpu.SemaphoreType.DMA((len(blocks),)),
            pltpu.SemaphoreType.DMA(()),
        ],
        input_output_aliases=aliases,
        compiler_params=pltpu.CompilerParams(vmem_limit_bytes=VMEM),
        cost_estimate=pl.CostEstimate(
            flops=2 * total * rows * share,
            bytes_accessed=2 * rows * share * (CAND + 1),
            transcendentals=rows * share,
        ),
    )(*operands)


def by_swaps(factors_in, factors_out, basis_in, basis_out, eigvals, live_counts):
    own = lax.axis_index("dp").astype(jnp.int32)[None]
    column = (0, 4, 8, 12)
    pair = (2, 6, 10, 14)
    core = (1, 5, 9, 13)
    other = (3, 7, 11, 15)
    tie = lax.optimization_barrier

    a2, a3 = [swap(factors_in, m) for m in (8, 12)]
    shape = (2,) + factors_in.shape
    plane, slot = [lax.broadcasted_iota(jnp.int32, shape, k) for k in (0, 1)]
    keep = (plane == 0) | (slot < live_counts[0])
    zero = jnp.zeros((), factors_in.dtype)
    f = tie(jnp.where(keep, jnp.stack([factors_in, factors_out]), zero))
    b2, b3 = [swap(f[1], m) for m in (8, 12)]
    f1, fp = tie((swap(f, 4), swap(f, 2)))
    fp1 = swap(f1, 2)
    a2, a3 = tie((a2, a3))[:2]
    a_far = jnp.stack([a2, a3])
    a_far_pair = swap(a_far, 2)
    a_far_core = swap(a_far, 1)
    near = jnp.stack([f, f1, fp, fp1])
    near_core = swap(near, 1)
    a_far_other = swap(a_far_pair, 1)
    a_far_other, b2, b3 = tie((a_far_other, b2, b3))
    b_far = jnp.stack([b2, b3])
    b_far_pair = swap(b_far, 2)
    joined = [(near, (0, 4, 2, 6)), (near_core, (1, 5, 3, 7))]
    pin = project(
        own,
        joined + [
            (a_far, column[2:]), (a_far_pair, pair[2:]), (a_far_core, core[2:]),
            (a_far_other, other[2:]),
        ],
        basis_in, 0, False,
    )

    b_far_pair = after(b_far_pair, pin)
    b_far = jnp.concatenate([b_far, b_far_pair])
    b_far_core = swap(b_far, 1)
    blocks = joined + [(b_far, column[2:] + pair[2:]), (b_far_core, core[2:] + other[2:])]
    g1, g2, g3 = [swap(pin, m) for m in (4, 8, 12)]
    left = project(own, blocks, basis_out, 1, True)
    g1, g2, g3 = tie((g1, g2, g3, left))[:3]
    g_column = jnp.stack([pin, g1, g2, g3])
    g_pair = swap(g_column, 2)
    out = outer(own, [(g_column, column)], left, eigvals, None)
    g_core = swap(after(g_column, out), 1)
    g_other = swap(after(g_pair, out), 1)
    return outer(own, [(g_core, core), (g_pair, pair), (g_other, other)], left, eigvals, out)


def solution(mesh):
    placed = (
        P(("groups", "dp"), "basis"),
        P(("groups", "dp"), "basis"),
        P("basis", "dp"),
        P("basis", "dp"),
        P("dp", None),
        P(("groups", "dp")),
    )
    chosen = by_swaps if mesh.shape["basis"] == 1 and mesh.shape["dp"] == 16 else general
    return jax.shard_map(
        chosen,
        mesh=mesh,
        in_specs=placed,
        out_specs=P(("groups", "basis"), "dp", None),
        check_vma=False,
    )
```

```python
import functools

import jax
import jax.numpy as jnp
from jax import lax
from jax.experimental import pallas as pl
from jax.experimental.pallas import tpu as pltpu
from jax.sharding import PartitionSpec as P

CAND = 4
KBLK = 1024
RBLK = 256
FLIGHT = 4
VMEM = 50 << 20


def general(factors_in, factors_out, basis_in, basis_out, eigvals, live_counts):
    slot_rows = factors_in.shape[0]
    keep = (lax.iota(jnp.int32, slot_rows) < live_counts[0])[:, None]
    masked = jnp.where(keep, factors_in, jnp.zeros_like(factors_in))
    partial_in = jnp.dot(
        lax.all_gather(masked, "dp", axis=0, tiled=True),
        basis_in,
        preferred_element_type=jnp.float32,
    )
    partial_out = jnp.dot(
        lax.all_gather(factors_out, "dp", axis=0, tiled=True),
        basis_out,
        preferred_element_type=jnp.float32,
    )
    halves = lax.axis_size("basis")
    share = partial_in.shape[0] // halves
    summed_in, summed_out = lax.psum((partial_in, partial_out), "basis")
    first = lax.axis_index("basis") * share
    proj_in = lax.dynamic_slice_in_dim(summed_in, first, share, 0).astype(jnp.bfloat16)
    proj_out = lax.dynamic_slice_in_dim(summed_out, first, share, 0).astype(jnp.bfloat16)
    cand_local = CAND // halves
    per_cand = share // cand_local
    pout_grouped = proj_out.reshape(cand_local, per_cand, proj_out.shape[1])
    shifted = eigvals.astype(jnp.float32) + 0.01
    piece = lax.all_gather(proj_in, "dp", axis=1, tiled=True)
    pin_grouped = piece.reshape(cand_local, per_cand, piece.shape[1])
    summed = jnp.einsum(
        "ati,atj->aij", pout_grouped, pin_grouped, preferred_element_type=jnp.float32
    )
    return (summed / shifted[None, :, :]).astype(jnp.bfloat16)


def swap(x, m):
    n = lax.axis_size("dp")
    return lax.ppermute(x, "dp", [(d, d ^ m) for d in range(n)])


def after(x, *others):
    return lax.optimization_barrier((x,) + others)[0]


def project_kernel(blocks, which, turn, own_ref, *refs):
    count = len(blocks)
    sources, basis_ref, out_ref = refs[:count], refs[count], refs[count + 1]
    pieces, (held, rows, sems, piece_sems) = refs[count + 2:-4], refs[-4:]
    chunks, width = held.shape[:2]
    slots = pieces[0].shape[-2]
    copies = [
        pltpu.make_async_copy(
            source if len(source.shape) == 3 else source.at[:, which], piece, piece_sems.at[k]
        )
        for k, (source, piece) in enumerate(zip(sources, pieces))
    ]
    reads = [
        pltpu.make_async_copy(basis_ref.at[pl.ds(k * width, width)], held.at[k], sems.at[k])
        for k in range(chunks)
    ]
    reads[0].start()
    for copy in copies:
        copy.start()
    for read in reads[1:]:
        read.start()
    for copy in copies:
        copy.wait()
    acc = None
    for k in range(chunks):
        part = slice(k * width, (k + 1) * width)
        for piece, entries in zip(pieces, blocks):
            for e, m in enumerate(entries):
                rows[m * slots:(m + 1) * slots, part] = piece[e, :, part].astype(jnp.float32)
        reads[k].wait()
        part = jnp.dot(
            rows[:, part].astype(jnp.bfloat16),
            held[k],
            preferred_element_type=jnp.float32,
        )
        acc = part if acc is None else acc + part
    total = rows.shape[0]
    to = lax.broadcasted_iota(jnp.int32, (total, total), 0)
    come = lax.broadcasted_iota(jnp.int32, (total, total), 1)
    where = jnp.bitwise_xor(come // slots, own_ref[0]) * slots + come % slots
    pick = jnp.where(to == where, 1.0, 0.0).astype(jnp.bfloat16)
    proj = jnp.dot(pick, acc.astype(jnp.bfloat16), preferred_element_type=jnp.float32)
    if turn:
        turned = proj.T
        token = lax.broadcasted_iota(jnp.int32, turned.shape, 1)
        for c in range(CAND):
            own_tokens = token // (total // CAND) == c
            out_ref[c] = jnp.where(own_tokens, turned, 0.0).astype(jnp.bfloat16)
    else:
        out_ref[...] = proj.astype(jnp.bfloat16)


def anywhere(count):
    return [pl.BlockSpec(memory_space=pl.ANY)] * count


def project(own, blocks, basis, which, turn):
    slots = blocks[0][0].shape[-2]
    depth, cols = basis.shape
    total = slots * sum(len(entries) for _, entries in blocks)
    shape = (CAND, cols, total) if turn else (total, cols)
    chunks = depth // KBLK
    return pl.pallas_call(
        functools.partial(project_kernel, [entries for _, entries in blocks], which, turn),
        out_shape=jax.ShapeDtypeStruct(shape, jnp.bfloat16),
        in_specs=[pl.BlockSpec(memory_space=pltpu.SMEM)] + anywhere(len(blocks) + 1),
        out_specs=pl.BlockSpec(memory_space=pltpu.VMEM),
        scratch_shapes=[
            pltpu.VMEM((len(entries), slots, depth), jnp.bfloat16) for _, entries in blocks
        ] + [
            pltpu.VMEM((chunks, KBLK, cols), jnp.bfloat16),
            pltpu.VMEM((total, depth), jnp.float32),
            pltpu.SemaphoreType.DMA((chunks,)),
            pltpu.SemaphoreType.DMA((len(blocks),)),
        ],
        compiler_params=pltpu.CompilerParams(vmem_limit_bytes=VMEM),
        cost_estimate=pl.CostEstimate(flops=total, bytes_accessed=total, transcendentals=0),
    )(own, *[x for x, _ in blocks], basis)


def outer_kernel(blocks, own_ref, *refs):
    given = len(blocks)
    sources, left_any, eig_ref = refs[:given], refs[given], refs[given + 1]
    out_ref, left, right, eig, out, eig_sems, out_sems, piece_sems, left_sem = refs[-9:]
    order = [m for entries in blocks for m in entries]
    count = len(order)
    rows, cols = eig.shape[1:]
    depth = out.shape[0]

    def columns(s):
        m = jnp.int32(order[0])
        for k in range(1, count):
            m = jnp.where(s == k, order[k], m)
        return pl.ds(pl.multiple_of(jnp.bitwise_xor(m, own_ref[0]) * cols, cols), cols)

    def read(s):
        return pltpu.make_async_copy(eig_ref.at[:, columns(s)], eig.at[s], eig_sems.at[s])

    def write(s, r, c):
        slot, part = lax.rem(s, depth), pl.ds(r, RBLK)
        return pltpu.make_async_copy(
            out.at[slot, c, part],
            out_ref.at[c, part, columns(s)],
            out_sems.at[slot, r // RBLK, c],
        )

    parts = [(r, c) for r in range(0, rows, RBLK) for c in range(CAND)]

    copies, at = [pltpu.make_async_copy(left_any, left, left_sem)], 0
    for k, (source, entries) in enumerate(zip(sources, blocks)):
        room = right.at[pl.ds(at, len(entries))]
        copies.append(pltpu.make_async_copy(source, room, piece_sems.at[k]))
        at += len(entries)
    read(0).start()
    for copy in copies:
        copy.start()
    for s in range(1, count):
        read(s).start()
    for copy in copies:
        copy.wait()

    def work(s, slot):
        read(s).wait()
        for r in range(0, rows, RBLK):
            shifted = eig[s, r:r + RBLK, :].astype(jnp.float32) + 0.01
            near = pl.reciprocal(shifted, approx=True)
            scale = near * (2.0 - shifted * near)
            for c in range(CAND):
                summed = jnp.dot(
                    left[c, r:r + RBLK, :], right[s], preferred_element_type=jnp.float32
                )
                out[slot, c, r:r + RBLK, :] = (summed * scale).astype(jnp.bfloat16)
            for c in range(CAND):
                write(s, r, c).start()

    for s in range(depth):
        work(s, s)

    @pl.loop(depth, count)
    def _(s):
        for r, c in parts:
            write(s - depth, r, c).wait()
        work(s, lax.rem(s, depth))

    for s in range(max(0, count - depth), count):
        for r, c in parts:
            write(s, r, c).wait()


def outer(own, blocks, left, eigvals, before):
    total, cols = blocks[0][0].shape[-2:]
    rows, width = eigvals.shape
    count = sum(len(entries) for _, entries in blocks)
    operands = [own] + [x for x, _ in blocks] + [left, eigvals]
    aliases = {}
    if before is not None:
        aliases = {len(operands): 0}
        operands.append(before)
    share = count * cols
    return pl.pallas_call(
        functools.partial(outer_kernel, [entries for _, entries in blocks]),
        out_shape=jax.ShapeDtypeStruct((CAND, rows, width), jnp.bfloat16),
        in_specs=[pl.BlockSpec(memory_space=pltpu.SMEM)] + anywhere(len(operands) - 1),
        out_specs=pl.BlockSpec(memory_space=pl.ANY),
        scratch_shapes=[
            pltpu.VMEM(left.shape, jnp.bfloat16),
            pltpu.VMEM((count, total, cols), jnp.bfloat16),
            pltpu.VMEM((count, rows, cols), jnp.bfloat16),
            pltpu.VMEM((FLIGHT, CAND, rows, cols), jnp.bfloat16),
            pltpu.SemaphoreType.DMA((count,)),
            pltpu.SemaphoreType.DMA((FLIGHT, rows // RBLK, CAND)),
            pltpu.SemaphoreType.DMA((len(blocks),)),
            pltpu.SemaphoreType.DMA(()),
        ],
        input_output_aliases=aliases,
        compiler_params=pltpu.CompilerParams(vmem_limit_bytes=VMEM),
        cost_estimate=pl.CostEstimate(
            flops=2 * total * rows * share,
            bytes_accessed=2 * rows * share * (CAND + 1),
            transcendentals=rows * share,
        ),
    )(*operands)


def by_swaps(factors_in, factors_out, basis_in, basis_out, eigvals, live_counts):
    own = lax.axis_index("dp").astype(jnp.int32)[None]
    column = (0, 4, 8, 12)
    pair = (2, 6, 10, 14)
    core = (1, 5, 9, 13)
    other = (3, 7, 11, 15)
    tie = lax.optimization_barrier

    a2, a3 = [swap(factors_in, m) for m in (8, 12)]
    shape = (2,) + factors_in.shape
    plane, slot = [lax.broadcasted_iota(jnp.int32, shape, k) for k in (0, 1)]
    keep = (plane == 0) | (slot < live_counts[0])
    zero = jnp.zeros((), factors_in.dtype)
    f = tie(jnp.where(keep, jnp.stack([factors_in, factors_out]), zero))
    b2, b3 = [swap(f[1], m) for m in (8, 12)]
    f1, fp = tie((swap(f, 4), swap(f, 2)))
    fp1 = swap(f1, 2)
    a2, a3 = tie((a2, a3))[:2]
    a_far = jnp.stack([a2, a3])
    a_far_pair = swap(a_far, 2)
    a_far_core = swap(a_far, 1)
    near = jnp.stack([f, f1, fp, fp1])
    near_core = swap(near, 1)
    a_far_other = swap(a_far_pair, 1)
    a_far_other, b2, b3 = tie((a_far_other, b2, b3))
    b_far = jnp.stack([b2, b3])
    b_far_pair = swap(b_far, 2)
    joined = [(near, (0, 4, 2, 6)), (near_core, (1, 5, 3, 7))]
    pin = project(
        own,
        joined + [
            (a_far, column[2:]), (a_far_pair, pair[2:]), (a_far_core, core[2:]),
            (a_far_other, other[2:]),
        ],
        basis_in, 0, False,
    )

    b_far_pair = after(b_far_pair, pin)
    b_far = jnp.concatenate([b_far, b_far_pair])
    b_far_core = swap(b_far, 1)
    blocks = joined + [(b_far, column[2:] + pair[2:]), (b_far_core, core[2:] + other[2:])]
    g1, g2, g3 = [swap(pin, m) for m in (4, 8, 12)]
    left = project(own, blocks, basis_out, 1, True)
    g1, g2, g3 = tie((g1, g2, g3, left))[:3]
    g_column = jnp.stack([pin, g1, g2, g3])
    g_pair = swap(g_column, 2)
    out = outer(own, [(g_column, column)], left, eigvals, None)
    g_core = swap(after(g_column, out), 1)
    g_other = swap(after(g_pair, out), 1)
    return outer(own, [(g_core, core), (g_pair, pair), (g_other, other)], left, eigvals, out)


def solution(mesh):
    placed = (
        P(("groups", "dp"), "basis"),
        P(("groups", "dp"), "basis"),
        P("basis", "dp"),
        P("basis", "dp"),
        P("dp", None),
        P(("groups", "dp")),
    )
    chosen = by_swaps if mesh.shape["basis"] == 1 and mesh.shape["dp"] == 16 else general
    return jax.shard_map(
        chosen,
        mesh=mesh,
        in_specs=placed,
        out_specs=P(("groups", "basis"), "dp", None),
        check_vma=False,
    )
```
